32 devices in a mesh: ens: 2 (over x), space: 8 (over z, y), tm: 2 (over core).
Axes of the slice: x: 2, y: 2, z: 4, core: 2. Of those that a mesh axis runs over, the one named last changes fastest.
Arguments:
- adjoint_in: float32 [4, 3, 3, 64, 2048], P(('ens', 'tm'), None, None, 'space'), parts along dimension 0, may hold values from -6 to 6
- layer_depth: float32 [3, 64, 2048], P(None, 'space'), may hold values from 0.5 to 2
- obs_cell: int32 [4, 131072], P(('ens', 'tm'), 'space'), parts along dimension 0, may hold values from 0 to 16383
- obs_plane: int32 [4, 131072], P(('ens', 'tm'), 'space'), parts along dimension 0, may hold values from 0 to 11
- obs_owner: int32 [4, 131072, 1], P(('ens', 'tm'), 'space'), parts along dimension 0, may hold values from 0 to 7; in each aligned block of 16384 rows (0 to 16383, 16384 to 32767, ..., all dimensions but the last counted through in order) at most 2560 rows name the same one
- innovation: float32 [4, 131072], P(('ens', 'tm'), 'space'), parts along dimension 0, may hold values from -6 to 6
- obs_weight: float32 [4, 4, 131072], P(None, ('ens', 'tm'), 'space'), parts along dimension 1, may hold values from 0 to 1
- obs_count: int32 [4, 8], P(('ens', 'tm'), 'space'), parts along dimension 0, may hold values from 1 to 16384, 98304 in all within a row
Outputs:
- adjoint_out: float32 [4, 3, 3, 64, 2048], P(('ens', 'tm'), None, None, 'space'), parts along dimension 0
The draws below stay inside these ranges and needn't reach their ends.
There are 2 independent parts, one for each index of `ens`. The reference program is written for one: setup_inputs(seed, part) draws one part's arguments, and reference() takes and returns one part's arrays. A program takes and returns all parts, laid end to end along the dimension named above; an argument that names none is the same for every part. Nothing has to cross between parts.
Inputs may be any that keep to these rules, and one draw needn't show every extreme that they name: `obs_owner`: among the 16384 rows of one tile in one sub-window at most 2560 name the same owner tile; some owner is named by exactly 2560 of them. `obs_cell`: the cell lies inside the owner tile; its lower and right neighbours may lie in the next tile or wrap around. `obs_count`: the live rows of a tile are its first ones; the counts of one sub-window sum to 98304 and the largest is 16384.
All inputs are finite; a program needn't handle non-finite values. No bound on the sum of `obs_count` on one device may be relied on, other than what follows from the above.
Results may differ from the reference program's by a relative error of at most 0.000037.
Values sent between devices are 32-bit elements; how exact they have to be, the bound alone decides.
A program may use at most 64 MiB of HBM per device.

```python
import math
import jax
import jax.numpy as jnp
import numpy as np

LAYERS = 3
STEPS = 4
ROWS_DEV = 8
NY = 2048
OBS_DEV = 16384
SUBWIN = 2
NX = 64
OBS = 131072
CAP = 2560
N_SPACE = 8


def touch_ends(result, key, least, top_value):
    place = [jax.random.randint(jax.random.fold_in(key, axis), (), 0, length) for axis, length in enumerate(result.shape)]
    main_axis = result.shape.index(max(result.shape))
    next_to = place[:main_axis] + [(place[main_axis] + 1) % result.shape[main_axis]] + place[main_axis + 1:]
    return result.at[tuple(place)].set(least).at[tuple(next_to)].set(top_value)


def block_levels(rng, shape, pieces, least, largest):
    factor_of, own = 1.0, jax.random.fold_in(rng, 6)
    for dim, blocks in pieces:
        steps = jnp.exp(jax.random.uniform(jax.random.fold_in(own, dim), (blocks,), jnp.float32, least / len(pieces), largest / len(pieces)))
        factor_of = factor_of * jnp.repeat(steps, shape[dim] // blocks).reshape([-1 if axis == dim else 1 for axis in range(len(shape))])
    return factor_of


def split_up(amount, total, bound, skew):
    weights = [(1 << 20) // math.isqrt(rank ** skew) + 1 for rank in range(2, amount + 1)]
    rest, counts = total - bound - (amount - 1), [1] * (amount - 1)
    while rest > 0:
        free = [i for i in range(amount - 1) if counts[i] < bound]
        mass, left = sum([weights[i] for i in free]), rest
        for i in free:
            addition = min(bound - counts[i], max(1, left * weights[i] // mass), rest)
            counts[i] = counts[i] + addition
            rest = rest - addition
    return np.array([bound] + counts)


def uneven_parts(rng, number_of, total, limit, slope):
    if number_of == 2:
        one = jax.random.randint(rng, (), max(1, total - limit), min(limit, total - 1) + 1)
        return jnp.stack([one, total - one])
    lengths = jnp.asarray(split_up(number_of, total, limit, slope), jnp.int32)
    pairs = (number_of - 1) // 2
    giver, taker = lengths[1:1 + 2 * pairs:2], lengths[2:2 + 2 * pairs:2]
    margin = jnp.minimum(giver - 1, limit - taker)
    passed = jax.random.randint(jax.random.fold_in(rng, 1), (pairs,), 0, 1 << 20) % (margin + 1)
    lengths = lengths.at[1:1 + 2 * pairs:2].set(giver - passed).at[2:2 + 2 * pairs:2].set(taker + passed)
    return lengths[jax.random.permutation(jax.random.fold_in(rng, 2), number_of)]


def deal_out(own_key, own, number, rows, count, top, limit, skew):
    ranking = jax.random.permutation(own_key, count)
    packed, common = load_shares(count, rows * top, limit, skew, True), load_shares(count, rows * top, limit, skew, False)
    places = jnp.arange(count)

    def named(lengths, turn):
        used = int((lengths > 0).sum())
        fixed = max(1, used // 4)
        shifted = fixed + (places - fixed + turn * (used - fixed)) % max(1, count - fixed)
        return jnp.zeros((count,), jnp.int32).at[ranking[jnp.where(places < fixed, places, shifted)]].set(jnp.asarray(lengths, jnp.int32))

    lengths = jnp.where(number % 4 == 0, named(packed, number // 4), named(common, number - number // 4 - 1))
    mixed = jax.random.permutation(jax.random.fold_in(own, 3), count)
    giver, receiver = mixed[0:count // 2 * 2:2], mixed[1:count // 2 * 2:2]
    slack = jnp.minimum(lengths[giver] - 1, limit - lengths[receiver]) // 2
    slack = jnp.where((giver == ranking[0]) | (receiver == ranking[0]) | (lengths[receiver] == 0), 0, jnp.maximum(slack, 0))
    shifted = jax.random.randint(jax.random.fold_in(own, 4), (count // 2,), 0, 1 << 20) % (slack + 1)
    lengths = lengths.at[giver].add(-shifted).at[receiver].add(shifted)
    labels = jnp.searchsorted(jnp.cumsum(lengths), jnp.arange(rows * top), side="right").astype(jnp.int32)
    listing = labels.reshape(top, rows).T
    listing = listing[jax.random.permutation(jax.random.fold_in(own, 1), rows)]
    turn = jax.random.randint(jax.random.fold_in(own, 2), (rows, 1), 0, top)
    return jnp.take_along_axis(listing, (jnp.arange(top)[None, :] + turn) % top, axis=1)


def load_shares(amount, total, reach, lean, full):
    weights = [(1 << 20) // math.isqrt(standing ** lean) + 1 for standing in range(1, amount + 1)]
    largest = reach if full else min(reach, max(-(-total // amount), total * weights[0] // sum(weights)))
    least = 1 if total - largest >= amount - 1 else 0
    counts, surplus = [largest] + [least] * (amount - 1), total - largest - least * (amount - 1)
    while surplus > 0:
        free = [i for i in range(1, amount) if counts[i] < largest] or [i for i in range(1, amount) if counts[i] < reach]
        mass, budget = sum([weights[i] for i in free]), surplus
        for i in free:
            more = min(reach - counts[i], max(1, budget * weights[i] // mass), surplus)
            counts[i] = counts[i] + more
            surplus = surplus - more
    return np.array(counts)


def scatter_about(key, dims, scale, limit, pieces=(), kind=jnp.bfloat16):
    values = jax.random.normal(key, dims, jnp.float32) * scale
    if len(pieces) > 0:
        values = block_levels(key, dims, pieces, -0.22, 0.18) * values
    return jnp.clip(values, min=-limit, max=limit).astype(kind)


def setup_inputs(seed: int = 0, part: int = 0) -> dict:
    arg_keys = jax.random.split(jax.random.key(seed), 9)
    part_keys = jax.random.split(jax.random.fold_in(arg_keys[8], part), 9)
    adjoint_in = scatter_about(part_keys[0], (SUBWIN, 3, LAYERS, NX, NY), 1.0, 6.0, ((0, 2), (3, 8)), jnp.float32)
    layer_depth = jnp.clip(jnp.exp(math.log(2.0) - 1.3862944 * jax.random.uniform(arg_keys[1], (LAYERS, NX, NY), jnp.float32) ** block_levels(arg_keys[1], (LAYERS, NX, NY), ((1, 8),), -0.2, 0.2)), 0.5, 2.0)
    obs_cell = touch_ends(jax.random.randint(part_keys[2], (SUBWIN, OBS), 0, ROWS_DEV * NY), jax.random.fold_in(part_keys[2], 1), 0, (ROWS_DEV * NY) - 1).astype(jnp.int32)
    obs_plane = touch_ends(jax.random.randint(part_keys[3], (SUBWIN, OBS), 0, STEPS * LAYERS), jax.random.fold_in(part_keys[3], 1), 0, (STEPS * LAYERS) - 1).astype(jnp.int32)
    obs_owner_keys = jax.random.split(jax.random.fold_in(part_keys[4], 1), SUBWIN * OBS // OBS_DEV)
    obs_owner_turns = jax.random.permutation(jax.random.fold_in(part_keys[4], 3), SUBWIN * OBS // OBS_DEV)
    obs_owner = jax.vmap(lambda own, number: deal_out(jax.random.fold_in(part_keys[4], 2), own, number, OBS_DEV, N_SPACE, 1, CAP, 2))(obs_owner_keys, obs_owner_turns).reshape((SUBWIN, OBS, 1))
    innovation = scatter_about(part_keys[5], (SUBWIN, OBS), 1.0, 6.0, ((0, 2), (1, 8)), jnp.float32)
    obs_weight = jnp.clip(1.0 * jax.random.uniform(part_keys[6], (4, SUBWIN, OBS), jnp.float32) ** block_levels(part_keys[6], (4, SUBWIN, OBS), ((1, 2), (2, 8)), -0.2, 0.2), 0.0, 1.0)
    obs_count = jax.vmap(lambda own: uneven_parts(own, N_SPACE, 3 * N_SPACE * OBS_DEV // 4, OBS_DEV, 2))(jax.random.split(part_keys[7], SUBWIN)).reshape((SUBWIN, N_SPACE)).astype(jnp.int32)
    return dict(adjoint_in=adjoint_in, layer_depth=layer_depth, obs_cell=obs_cell, obs_plane=obs_plane, obs_owner=obs_owner, innovation=innovation, obs_weight=obs_weight, obs_count=obs_count)


time_step = 0.4
friction = 0.05
coriolis_mid = 0.3
coriolis_slope = 0.2
coupling = ((1.0, 0.5, 0.25), (0.5, 1.0, 0.5), (0.25, 0.5, 1.0))


def couple_layers(field):
    return jnp.stack([coupling[0][m] * field[0] + coupling[1][m] * field[1] + coupling[2][m] * field[2] for m in range(3)])


def along_rows(field):
    return (jnp.roll(field, -1, axis=1) - jnp.roll(field, 1, axis=1)) * 0.5


def along_cols(field):
    return (jnp.roll(field, -1, axis=2) - jnp.roll(field, 1, axis=2)) * 0.5


def advance(adjoint, layer_depth, coriolis):
    height, east, north = adjoint[0], adjoint[1], adjoint[2]
    thick = layer_depth * height
    east_mix = couple_layers(east)
    north_mix = couple_layers(north)
    new_height = height + time_step * (along_rows(east_mix) + along_cols(north_mix))
    new_east = east + time_step * (along_rows(thick) - coriolis * north - friction * east)
    new_north = north + time_step * (along_cols(thick) + coriolis * east - friction * north)
    return jnp.stack([new_height, new_east, new_north])


def forcing_of(obs_cell, obs_plane, obs_owner, innovation, obs_weight, obs_count):
    position = jnp.arange(OBS, dtype=jnp.int32)
    tile_of = position // OBS_DEV
    is_live = (position % OBS_DEV) < obs_count[tile_of]
    weighted_base = innovation * is_live.astype(jnp.float32)
    plane = obs_plane
    grid_row = obs_owner[:, 0] * ROWS_DEV + obs_cell // NY
    column = obs_cell % NY
    next_row = (grid_row + 1) % NX
    next_col = (column + 1) % NY
    forcing = jnp.zeros((STEPS * LAYERS, NX, NY), jnp.float32)
    forcing = forcing.at[plane, grid_row, column].add(obs_weight[0] * weighted_base)
    forcing = forcing.at[plane, grid_row, next_col].add(obs_weight[1] * weighted_base)
    forcing = forcing.at[plane, next_row, column].add(obs_weight[2] * weighted_base)
    forcing = forcing.at[plane, next_row, next_col].add(obs_weight[3] * weighted_base)
    return forcing.reshape(STEPS, LAYERS, NX, NY)


def reference(adjoint_in, layer_depth, obs_cell, obs_plane, obs_owner, innovation, obs_weight, obs_count):
    coriolis = coriolis_mid + coriolis_slope * (jnp.arange(NY, dtype=jnp.float32) / NY - 0.5)
    results = []
    for window in range(SUBWIN):
        forcing = forcing_of(obs_cell[window], obs_plane[window], obs_owner[window], innovation[window], obs_weight[:, window], obs_count[window])
        if window + 1 < SUBWIN:
            adjoint = adjoint_in[window + 1]
        else:
            adjoint = jnp.zeros_like(adjoint_in[0])
        for step_index in reversed(range(STEPS)):
            adjoint = adjoint.at[0].add(forcing[step_index])
            adjoint = advance(adjoint, layer_depth, coriolis)
        results.append(adjoint_in[window] - adjoint)
    return jnp.stack(results)
```

```python
import functools

import jax
import jax.numpy as jnp
from jax import lax
from jax.experimental import pallas as pl
from jax.experimental.pallas import tpu as pltpu
from jax.sharding import PartitionSpec as P

STEPS = 4
LANES = 128
WINDOW = 256
FIELDS = 6

time_step = 0.4
friction = 0.05
coriolis_mid = 0.3
coriolis_slope = 0.2
coupling = ((1.0, 0.5, 0.25), (0.5, 1.0, 0.5), (0.25, 0.5, 1.0))

NT = (((1,), (1,)), ((), ()))


def padded(block, sides, width):
    for axis, dim in sides:
        count = lax.axis_size(axis)
        forward = [(i, i + 1) for i in range(count - 1)]
        forward.append((count - 1, 0))
        backward = [(target, source) for source, target in forward]
        low = lax.ppermute(
            lax.slice_in_dim(block, block.shape[dim] - width, None, axis=dim), axis, forward
        )
        high = lax.ppermute(lax.slice_in_dim(block, 0, width, axis=dim), axis, backward)
        block = jnp.concatenate([low, block, high], axis=dim)
    return block


def couple_layers(field):
    return jnp.stack(
        [
            coupling[0][m] * field[0] + coupling[1][m] * field[1] + coupling[2][m] * field[2]
            for m in range(3)
        ]
    )


def along_rows(field):
    return (field[:, 2:] - field[:, :-2]) * 0.5


def along_cols(field):
    interior = field[:, 1:-1]
    return (jnp.roll(interior, -1, axis=2) - jnp.roll(interior, 1, axis=2)) * 0.5


def advance(extended, depth_ext, coriolis, layer_count):
    height = extended[0:layer_count]
    east = extended[layer_count : 2 * layer_count]
    north = extended[2 * layer_count : 3 * layer_count]
    thick = depth_ext * height
    east_mix = couple_layers(east)
    north_mix = couple_layers(north)
    height_in = height[:, 1:-1]
    east_in = east[:, 1:-1]
    north_in = north[:, 1:-1]
    new_height = height_in + time_step * (along_rows(east_mix) + along_cols(north_mix))
    new_east = east_in + time_step * (along_rows(thick) - coriolis * north_in - friction * east_in)
    new_north = north_in + time_step * (
        along_cols(thick) + coriolis * east_in - friction * north_in
    )
    return jnp.concatenate([new_height, new_east, new_north], axis=0)


def spread(row, rows):
    part = jnp.broadcast_to(row, (16, row.shape[1])).astype(jnp.bfloat16)
    return jnp.concatenate([part] * (rows // 16), axis=0)


def one_hot(index_row, rows):
    places = lax.broadcasted_iota(jnp.int32, (rows, index_row.shape[1]), 0)
    return jnp.where(places == index_row, 1.0, 0.0)


def route_kernel(
    tiles,
    capacity,
    columns,
    tile_rows,
    width,
    count_ref,
    cell_ref,
    plane_ref,
    owner_ref,
    innov_ref,
    weight_ref,
    out_ref,
    key_ref,
    pos_ref,
    piece_ref,
    acc_ref,
):
    lines = cell_ref.shape[0]
    buckets = columns // WINDOW
    keys = tiles * buckets
    slot_rows = tiles * capacity // width
    place = lax.broadcasted_iota(jnp.int32, (lines, LANES), 0) * LANES + lax.broadcasted_iota(
        jnp.int32, (lines, LANES), 1
    )
    live = place < count_ref[0, 0]
    cell = cell_ref[...]
    column = jnp.bitwise_and(cell, columns - 1)
    row = jnp.right_shift(cell, columns.bit_length() - 1)
    bucket = jnp.right_shift(column, WINDOW.bit_length() - 1)
    key_ref[...] = jnp.where(live, owner_ref[...] * buckets + bucket, keys)
    piece_ref[0] = (plane_ref[...] * tile_rows + row + 1).astype(jnp.float32)
    piece_ref[1] = (bucket * WINDOW).astype(jnp.float32)
    piece_ref[2] = jnp.bitwise_and(column, WINDOW - 1).astype(jnp.float32)
    innovation = innov_ref[...]
    for corner in range(4):
        value = weight_ref[corner] * innovation
        high = value.astype(jnp.bfloat16).astype(jnp.float32)
        piece_ref[3 + 2 * corner] = high
        piece_ref[4 + 2 * corner] = value - high

    def count_step(line, total):
        for extra in range(8):
            total += one_hot(key_ref[pl.ds(line * 8 + extra, 1), :], keys)
        return total

    total = lax.fori_loop(0, lines // 8, count_step, jnp.zeros((keys, LANES), jnp.float32))
    mine = lax.broadcasted_iota(jnp.int32, (keys, keys), 0)
    other = lax.broadcasted_iota(jnp.int32, (keys, keys), 1)
    shift = buckets.bit_length() - 1
    same_owner = jnp.right_shift(mine, shift) == jnp.right_shift(other, shift)
    before = jnp.where(same_owner & (other < mine), 1.0, 0.0).astype(jnp.bfloat16)
    ahead = jnp.dot(before, total.astype(jnp.bfloat16), preferred_element_type=jnp.float32)
    owner_of = jnp.right_shift(lax.broadcasted_iota(jnp.int32, (keys, 1), 0), shift)
    base = jnp.sum(ahead, axis=1, keepdims=True) + (owner_of * capacity).astype(jnp.float32)
    triangle = jnp.where(
        lax.broadcasted_iota(jnp.int32, (256, 256), 0)
        < lax.broadcasted_iota(jnp.int32, (256, 256), 1),
        1.0,
        0.0,
    ).astype(jnp.bfloat16)

    def rank_step(step, base):
        for extra in range(4):
            line = step * 8 + extra * 2
            key = jnp.concatenate(
                [key_ref[pl.ds(line, 1), :], key_ref[pl.ds(line + 1, 1), :]], axis=1
            )
            hits = one_hot(key, keys)
            earlier = jnp.dot(
                hits.astype(jnp.bfloat16), triangle, preferred_element_type=jnp.float32
            )
            position = jnp.sum(hits * (earlier + base), axis=0, keepdims=True).astype(jnp.int32)
            position = jnp.where(key < keys, position, -1)
            pos_ref[pl.ds(line, 1), :] = position[:, :LANES]
            pos_ref[pl.ds(line + 1, 1), :] = position[:, LANES:]
            base += jnp.sum(hits, axis=1, keepdims=True)
        return base

    lax.fori_loop(0, lines // 8, rank_step, base)
    acc_ref[...] = jnp.zeros_like(acc_ref)
    log_width = width.bit_length() - 1

    def move_step(step, carry):
        span = range(8)
        slots, lefts = [], []
        for extra in span:
            position = pos_ref[pl.ds(step * 8 + extra, 1), :]
            slots.append(one_hot(jnp.right_shift(position, log_width), slot_rows).astype(jnp.bfloat16))
            lefts.append(one_hot(jnp.bitwise_and(position, width - 1), width).astype(jnp.bfloat16))
        lane_hits = jnp.concatenate(lefts, axis=1)
        for piece in range(11):
            part = jnp.concatenate(
                [
                    slots[extra] * spread(piece_ref[piece, pl.ds(step * 8 + extra, 1), :], slot_rows)
                    for extra in span
                ],
                axis=1,
            )
            field = 0 if piece == 0 else (piece + 1) // 2
            acc_ref[field] += lax.dot_general(
                part, lane_hits, NT, preferred_element_type=jnp.float32
            )
        return carry

    lax.fori_loop(0, lines // 8, move_step, 0)
    per_owner = capacity // width
    for owner in range(tiles):
        for field in range(FIELDS):
            out_ref[owner, field * per_owner : (field + 1) * per_owner, :] = acc_ref[
                field, owner * per_owner : (owner + 1) * per_owner, :
            ]


def route(cell, plane, owner, innovation, weights, count, tiles, capacity, columns, tile_rows):
    lines = cell.shape[0]
    width = 256 if capacity % 256 == 0 else LANES
    slot_rows = tiles * capacity // width
    vmem = pl.BlockSpec(memory_space=pltpu.VMEM)
    return pl.pallas_call(
        functools.partial(route_kernel, tiles, capacity, columns, tile_rows, width),
        out_shape=jax.ShapeDtypeStruct((tiles, FIELDS * (capacity // width), width), jnp.float32),
        in_specs=[pl.BlockSpec(memory_space=pltpu.SMEM)] + [vmem] * 5,
        out_specs=vmem,
        scratch_shapes=[
            pltpu.VMEM((lines, LANES), jnp.int32),
            pltpu.VMEM((lines, LANES), jnp.int32),
            pltpu.VMEM((11, lines, LANES), jnp.float32),
            pltpu.VMEM((FIELDS, slot_rows, width), jnp.float32),
        ],
        compiler_params=pltpu.CompilerParams(vmem_limit_bytes=48 * 1024 * 1024),
        name="route",
    )(count, cell, plane, owner, innovation, weights)


def force_kernel(planes, tile_rows, columns, low_ref, high_ref, in_ref, out_ref, carry_ref, acc_ref):
    tiles, depth, width = in_ref.shape
    per_tile = depth // FIELDS
    cells = planes * tile_rows
    acc_ref[...] = jnp.zeros_like(acc_ref)

    def source_step(source, carry):
        def block_step(block, carry):
            def field(number):
                return in_ref[source, pl.ds(number * per_tile + block, 1), :]

            line = field(0).astype(jnp.int32) - 1
            column = field(1).astype(jnp.int32)
            line_hits = one_hot(line, cells).astype(jnp.bfloat16)
            highs, lows = [], []
            for corner in range(4):
                value = field(2 + corner)
                high = value.astype(jnp.bfloat16).astype(jnp.float32)
                highs.append(line_hits * spread(high, cells))
                lows.append(line_hits * spread(value - high, cells))
            left = jnp.concatenate(
                [jnp.concatenate(highs, axis=0), jnp.concatenate(lows, axis=0)], axis=1
            )

            def window_step(window, carry):
                hits = one_hot(column - window * WINDOW, WINDOW).astype(jnp.bfloat16)
                right = jnp.concatenate([hits, hits], axis=1)
                acc_ref[window] += lax.dot_general(
                    left, right, NT, preferred_element_type=jnp.float32
                )
                return carry

            number = source * per_tile + block
            lax.fori_loop(low_ref[number], high_ref[number] + 1, window_step, 0)
            return carry

        return lax.fori_loop(0, per_tile, block_step, carry)

    lax.fori_loop(0, tiles, source_step, 0)
    row = lax.broadcasted_iota(jnp.int32, (tile_rows, columns), 0)
    for plane in range(planes):

        def gathered(corner):
            first = corner * cells + plane * tile_rows
            return jnp.concatenate(
                [acc_ref[w, first : first + tile_rows, :] for w in range(columns // WINDOW)],
                axis=1,
            )

        here = gathered(0) + pltpu.roll(gathered(1), 1, axis=1)
        below = gathered(2) + pltpu.roll(gathered(3), 1, axis=1)
        below = pltpu.roll(below, 1, axis=0)
        out_ref[plane] = here + jnp.where(row > 0, below, 0.0)
        carry_ref[plane] = jnp.where(row == 0, below, 0.0)


def force(arrived, planes, tile_rows, columns):
    tiles, depth, width = arrived.shape
    per_tile = depth // FIELDS
    line = arrived[:, :per_tile]
    column = arrived[:, per_tile : 2 * per_tile]
    low = jnp.min(jnp.where(line > 0, column, float(columns)), axis=2).reshape(tiles * per_tile)
    high = jnp.max(jnp.where(line > 0, column, -1.0), axis=2).reshape(tiles * per_tile)
    low = jnp.floor(low / WINDOW).astype(jnp.int32)
    high = jnp.floor(high / WINDOW).astype(jnp.int32)
    vmem = pl.BlockSpec(memory_space=pltpu.VMEM)
    smem = pl.BlockSpec(memory_space=pltpu.SMEM)
    shape = jax.ShapeDtypeStruct((planes, tile_rows, columns), jnp.float32)
    return pl.pallas_call(
        functools.partial(force_kernel, planes, tile_rows, columns),
        out_shape=(shape, shape),
        in_specs=[smem, smem, vmem],
        out_specs=(vmem, vmem),
        scratch_shapes=[
            pltpu.VMEM((columns // WINDOW, 4 * planes * tile_rows, WINDOW), jnp.float32)
        ],
        compiler_params=pltpu.CompilerParams(vmem_limit_bytes=48 * 1024 * 1024),
        name="force",
    )(low, high, arrived)


def body(
    adjoint_in, layer_depth, obs_cell, obs_plane, obs_owner, innovation, obs_weight, obs_count
):
    tiles = lax.axis_size("space")
    layer_count = layer_depth.shape[0]
    tile_rows = layer_depth.shape[1]
    columns = layer_depth.shape[2]
    obs_rows = obs_cell.shape[1]
    capacity = 5 * obs_rows // (4 * tiles)
    planes = STEPS * layer_count
    windows = lax.axis_size("tm")
    following = lax.ppermute(adjoint_in, "tm", [(i + 1, i) for i in range(windows - 1)])
    lines = obs_rows // LANES
    buffer = route(
        obs_cell.reshape(lines, LANES),
        obs_plane.reshape(lines, LANES),
        obs_owner.reshape(lines, LANES),
        innovation.reshape(lines, LANES),
        obs_weight.reshape(4, lines, LANES),
        obs_count,
        tiles,
        capacity,
        columns,
        tile_rows,
    )
    arrived = lax.all_to_all(buffer, "space", split_axis=0, concat_axis=0, tiled=True)
    forcing, spill = force(arrived, planes, tile_rows, columns)
    count = lax.axis_size("space")
    carried = lax.ppermute(spill[:, 0], "space", [(i, (i + 1) % count) for i in range(count)])
    forcing = forcing.at[:, 0, :].add(carried)
    coriolis = coriolis_mid + coriolis_slope * (
        jnp.arange(columns, dtype=jnp.float32) / columns - 0.5
    )
    adjoint = following[0].reshape(3 * layer_count, tile_rows, columns)
    depth_ext = padded(layer_depth, (("space", 1),), 1)
    current = adjoint
    for step_index in reversed(range(STEPS)):
        current = current.at[0:layer_count].add(
            forcing[step_index * layer_count : (step_index + 1) * layer_count]
        )
        extended = padded(current, (("space", 1),), 1)
        current = advance(extended, depth_ext, coriolis, layer_count)
    result = adjoint_in[0] - current.reshape(3, layer_count, tile_rows, columns)
    return result[None]


def solution(mesh):
    in_specs = (
        P(("ens", "tm"), None, None, "space", None),
        P(None, "space", None),
        P(("ens", "tm"), "space"),
        P(("ens", "tm"), "space"),
        P(("ens", "tm"), "space", None),
        P(("ens", "tm"), "space"),
        P(None, ("ens", "tm"), "space"),
        P(("ens", "tm"), "space"),
    )
    out_specs = P(("ens", "tm"), None, None, "space", None)
    return jax.shard_map(body, mesh=mesh, in_specs=in_specs, out_specs=out_specs, check_vma=False)
```

```python
import functools

import jax
import jax.numpy as jnp
from jax import lax
from jax.experimental import pallas as pl
from jax.experimental.pallas import tpu as pltpu
from jax.sharding import PartitionSpec as P

STEPS = 4
LANES = 128
WINDOW = 256
FIELDS = 6
GROUP = 4

time_step = 0.4
friction = 0.05
coriolis_mid = 0.3
coriolis_slope = 0.2
coupling = ((1.0, 0.5, 0.25), (0.5, 1.0, 0.5), (0.25, 0.5, 1.0))

NT = (((1,), (1,)), ((), ()))


def spread(row, rows):
    part = jnp.broadcast_to(row, (16, row.shape[1])).astype(jnp.bfloat16)
    return jnp.concatenate([part] * (rows // 16), axis=0)


def one_hot(index_row, rows):
    places = lax.broadcasted_iota(jnp.int32, (rows, index_row.shape[1]), 0)
    return jnp.where(places == index_row, 1.0, 0.0)


def route_kernel(
    tiles,
    capacity,
    columns,
    tile_rows,
    width,
    count_ref,
    cell_ref,
    plane_ref,
    owner_ref,
    innov_ref,
    weight_ref,
    out_ref,
    key_ref,
    pos_ref,
    piece_ref,
    acc_ref,
):
    lines = cell_ref.shape[0]
    buckets = columns // WINDOW
    keys = tiles * buckets
    slot_rows = tiles * capacity // width
    place = lax.broadcasted_iota(jnp.int32, (lines, LANES), 0) * LANES + lax.broadcasted_iota(
        jnp.int32, (lines, LANES), 1
    )
    live = place < count_ref[0, 0]
    cell = cell_ref[...]
    column = jnp.bitwise_and(cell, columns - 1)
    row = jnp.right_shift(cell, columns.bit_length() - 1)
    bucket = jnp.right_shift(column, WINDOW.bit_length() - 1)
    key_ref[...] = jnp.where(live, owner_ref[...] * buckets + bucket, keys)
    piece_ref[0] = (plane_ref[...] * tile_rows + row + 1).astype(jnp.float32)
    piece_ref[1] = (bucket * WINDOW).astype(jnp.float32)
    piece_ref[2] = jnp.bitwise_and(column, WINDOW - 1).astype(jnp.float32)
    innovation = innov_ref[...]
    for corner in range(4):
        value = weight_ref[corner] * innovation
        high = value.astype(jnp.bfloat16).astype(jnp.float32)
        piece_ref[3 + 2 * corner] = high
        piece_ref[4 + 2 * corner] = value - high

    def count_step(line, total):
        for extra in range(8):
            total += one_hot(key_ref[pl.ds(line * 8 + extra, 1), :], keys)
        return total

    total = lax.fori_loop(0, lines // 8, count_step, jnp.zeros((keys, LANES), jnp.float32))
    mine = lax.broadcasted_iota(jnp.int32, (keys, keys), 0)
    other = lax.broadcasted_iota(jnp.int32, (keys, keys), 1)
    shift = buckets.bit_length() - 1
    same_owner = jnp.right_shift(mine, shift) == jnp.right_shift(other, shift)
    before = jnp.where(same_owner & (other < mine), 1.0, 0.0).astype(jnp.bfloat16)
    ahead = jnp.dot(before, total.astype(jnp.bfloat16), preferred_element_type=jnp.float32)
    owner_of = jnp.right_shift(lax.broadcasted_iota(jnp.int32, (keys, 1), 0), shift)
    base = jnp.sum(ahead, axis=1, keepdims=True) + (owner_of * capacity).astype(jnp.float32)
    triangle = jnp.where(
        lax.broadcasted_iota(jnp.int32, (256, 256), 0)
        < lax.broadcasted_iota(jnp.int32, (256, 256), 1),
        1.0,
        0.0,
    ).astype(jnp.bfloat16)

    def rank_step(step, base):
        for extra in range(4):
            line = step * 8 + extra * 2
            key = jnp.concatenate(
                [key_ref[pl.ds(line, 1), :], key_ref[pl.ds(line + 1, 1), :]], axis=1
            )
            hits = one_hot(key, keys)
            earlier = jnp.dot(
                hits.astype(jnp.bfloat16), triangle, preferred_element_type=jnp.float32
            )
            position = jnp.sum(hits * (earlier + base), axis=0, keepdims=True).astype(jnp.int32)
            position = jnp.where(key < keys, position, -1)
            pos_ref[pl.ds(line, 1), :] = position[:, :LANES]
            pos_ref[pl.ds(line + 1, 1), :] = position[:, LANES:]
            base += jnp.sum(hits, axis=1, keepdims=True)
        return base

    lax.fori_loop(0, lines // 8, rank_step, base)
    acc_ref[...] = jnp.zeros_like(acc_ref)
    log_width = width.bit_length() - 1

    def move_step(step, carry):
        span = range(8)
        slots, lefts = [], []
        for extra in span:
            position = pos_ref[pl.ds(step * 8 + extra, 1), :]
            slots.append(one_hot(jnp.right_shift(position, log_width), slot_rows).astype(jnp.bfloat16))
            lefts.append(one_hot(jnp.bitwise_and(position, width - 1), width).astype(jnp.bfloat16))
        lane_hits = jnp.concatenate(lefts, axis=1)
        parts = []
        for extra in span:
            pieces = [
                slots[extra] * spread(piece_ref[piece, pl.ds(step * 8 + extra, 1), :], slot_rows)
                for piece in range(11)
            ]
            parts.append(jnp.concatenate(pieces, axis=0))
        acc_ref[...] += lax.dot_general(
            jnp.concatenate(parts, axis=1), lane_hits, NT, preferred_element_type=jnp.float32
        )
        return carry

    lax.fori_loop(0, lines // 8, move_step, 0)
    per_owner = capacity // width
    for owner in range(tiles):
        for field in range(FIELDS):

            def piece_rows(piece):
                first = piece * slot_rows + owner * per_owner
                return acc_ref[first : first + per_owner, :]

            value = piece_rows(0) if field == 0 else piece_rows(2 * field - 1) + piece_rows(2 * field)
            out_ref[owner, field * per_owner : (field + 1) * per_owner, :] = value


def route(cell, plane, owner, innovation, weights, count, tiles, capacity, columns, tile_rows):
    lines = cell.shape[0]
    width = 256 if capacity % 256 == 0 else LANES
    slot_rows = tiles * capacity // width
    vmem = pl.BlockSpec(memory_space=pltpu.VMEM)
    return pl.pallas_call(
        functools.partial(route_kernel, tiles, capacity, columns, tile_rows, width),
        out_shape=jax.ShapeDtypeStruct((tiles, FIELDS * (capacity // width), width), jnp.float32),
        in_specs=[pl.BlockSpec(memory_space=pltpu.SMEM)] + [vmem] * 5,
        out_specs=vmem,
        scratch_shapes=[
            pltpu.VMEM((lines, LANES), jnp.int32),
            pltpu.VMEM((lines, LANES), jnp.int32),
            pltpu.VMEM((11, lines, LANES), jnp.float32),
            pltpu.VMEM((11 * slot_rows, width), jnp.float32),
        ],
        compiler_params=pltpu.CompilerParams(vmem_limit_bytes=48 * 1024 * 1024),
        name="route",
    )(count, cell, plane, owner, innovation, weights)


def force_kernel(
    planes, tile_rows, columns, low_ref, high_ref, in_ref, out_ref, spill_ref, acc_ref, item_ref
):
    tiles, depth, width = in_ref.shape
    per_tile = depth // FIELDS
    cells = planes * tile_rows
    windows = columns // WINDOW
    acc_ref[...] = jnp.zeros_like(acc_ref)

    def list_source(source, count):
        def list_block(block, count):
            number = source * per_tile + block

            def list_window(window, count):
                item_ref[0, count] = source
                item_ref[1, count] = block
                item_ref[2, count] = window
                item_ref[3, count] = window
                return count + 1

            return lax.fori_loop(low_ref[number], high_ref[number] + 1, list_window, count)

        return lax.fori_loop(0, per_tile, list_block, count)

    count = lax.fori_loop(0, tiles, list_source, 0)
    for extra in range(GROUP):
        item_ref[0, count + extra] = 0
        item_ref[1, count + extra] = 0
        item_ref[2, count + extra] = windows
        item_ref[3, count + extra] = 0

    def product(item):
        source, block = item_ref[0, item], item_ref[1, item]

        def field(number):
            return in_ref[source, pl.ds(number * per_tile + block, 1), :]

        line = field(0).astype(jnp.int32) - 1
        column = field(1).astype(jnp.int32)
        line_hits = one_hot(line, cells).astype(jnp.bfloat16)
        highs, lows = [], []
        for corner in range(4):
            value = field(2 + corner)
            high = value.astype(jnp.bfloat16).astype(jnp.float32)
            highs.append(line_hits * spread(high, cells))
            lows.append(line_hits * spread(value - high, cells))
        left = jnp.concatenate(
            [jnp.concatenate(highs, axis=0), jnp.concatenate(lows, axis=0)], axis=1
        )
        hits = one_hot(column - item_ref[2, item] * WINDOW, WINDOW).astype(jnp.bfloat16)
        right = jnp.concatenate([hits, hits], axis=1)
        return lax.dot_general(left, right, NT, preferred_element_type=jnp.float32)

    def group_step(group, carry):
        found = [product(group * GROUP + extra) for extra in range(GROUP)]
        for extra in range(GROUP):
            acc_ref[item_ref[3, group * GROUP + extra]] += found[extra]
        return carry

    lax.fori_loop(0, (count + GROUP - 1) // GROUP, group_step, 0)
    row = lax.broadcasted_iota(jnp.int32, (tile_rows, columns), 0)
    for plane in range(planes):

        def gathered(corner):
            first = corner * cells + plane * tile_rows
            return jnp.concatenate(
                [acc_ref[w, first : first + tile_rows, :] for w in range(columns // WINDOW)],
                axis=1,
            )

        here = gathered(0) + pltpu.roll(gathered(1), 1, axis=1)
        below = gathered(2) + pltpu.roll(gathered(3), 1, axis=1)
        below = pltpu.roll(below, 1, axis=0)
        out_ref[plane] = here + jnp.where(row > 0, below, 0.0)
        spill_ref[plane : plane + 1, :] = below[0:1, :]


def force(arrived, planes, tile_rows, columns):
    tiles, depth, width = arrived.shape
    per_tile = depth // FIELDS
    line = arrived[:, :per_tile]
    column = arrived[:, per_tile : 2 * per_tile]
    low = jnp.min(jnp.where(line > 0, column, float(columns)), axis=2).reshape(tiles * per_tile)
    high = jnp.max(jnp.where(line > 0, column, -1.0), axis=2).reshape(tiles * per_tile)
    low = jnp.floor(low / WINDOW).astype(jnp.int32)
    high = jnp.floor(high / WINDOW).astype(jnp.int32)
    vmem = pl.BlockSpec(memory_space=pltpu.VMEM)
    smem = pl.BlockSpec(memory_space=pltpu.SMEM)
    shape = jax.ShapeDtypeStruct((planes, tile_rows, columns), jnp.float32)
    return pl.pallas_call(
        functools.partial(force_kernel, planes, tile_rows, columns),
        out_shape=(shape, jax.ShapeDtypeStruct((planes, columns), jnp.float32)),
        in_specs=[smem, smem, vmem],
        out_specs=(vmem, vmem),
        scratch_shapes=[
            pltpu.VMEM((columns // WINDOW, 4 * planes * tile_rows, WINDOW), jnp.float32),
            pltpu.SMEM((4, tiles * (per_tile * 2 + 2 * columns // WINDOW) + GROUP), jnp.int32),
        ],
        compiler_params=pltpu.CompilerParams(vmem_limit_bytes=48 * 1024 * 1024),
        name="force",
    )(low, high, arrived)


def stencil_kernel(
    adjoint_ref,
    depth_ref,
    forcing_ref,
    spill_ref,
    out_ref,
    edge_out,
    edge_in,
    depth_out,
    depth_in,
    spill_in,
    send_sem,
    recv_sem,
):
    layers, tile_rows, columns = depth_ref.shape
    tiles = lax.axis_size("space")
    me = lax.axis_index("space")
    after = lax.rem(me + 1, tiles)
    before = lax.rem(me + tiles - 1, tiles)
    barrier = pltpu.get_barrier_semaphore()
    for neighbour in (before, after):
        pl.semaphore_signal(
            barrier,
            inc=1,
            device_id={"space": neighbour},
            device_id_type=pl.DeviceIdType.MESH,
        )
    pl.semaphore_wait(barrier, 2)

    def copy(source, target, number, neighbour):
        return pltpu.make_async_remote_copy(
            src_ref=source,
            dst_ref=target,
            send_sem=send_sem.at[number],
            recv_sem=recv_sem.at[number],
            device_id={"space": neighbour},
            device_id_type=pl.DeviceIdType.MESH,
        )

    spill_copy = copy(spill_ref, spill_in, 2 * STEPS, after)
    depth_copy = copy(depth_out, depth_in, 2 * STEPS + 1, before)
    spill_copy.start()
    for layer in range(layers):
        depth_out[layer : layer + 1, :] = depth_ref[layer, 0:1, :]
    depth_copy.start()

    row = lax.broadcasted_iota(jnp.int32, (tile_rows, columns), 0)
    first, last = row == 0, row == tile_rows - 1
    place = lax.broadcasted_iota(jnp.int32, (tile_rows, columns), 1).astype(jnp.float32)
    coriolis = coriolis_mid + coriolis_slope * (place / columns - 0.5)
    half = 0.5 * time_step

    def rows_inside(field):
        ahead = jnp.where(last, 0.0, pltpu.roll(field, tile_rows - 1, axis=0))
        behind = jnp.where(first, 0.0, pltpu.roll(field, 1, axis=0))
        return ahead - behind

    def cols(field):
        return pltpu.roll(field, columns - 1, axis=1) - pltpu.roll(field, 1, axis=1)

    def mixed(fields, m):
        return sum(coupling[l][m] * fields[l] for l in range(3))

    copies = [spill_copy, depth_copy]
    for turn in range(STEPS):
        step = STEPS - 1 - turn
        state = adjoint_ref if turn == 0 else out_ref
        height = [state[l] + forcing_ref[step * layers + l] for l in range(layers)]
        if turn > 0:
            for l in range(layers):
                number = step * layers + l
                height[l] += jnp.where(first, spill_in[number : number + 1, :], 0.0)
        east = [state[layers + l] for l in range(layers)]
        north = [state[2 * layers + l] for l in range(layers)]
        east_mix = [mixed(east, m) for m in range(layers)]
        for l in range(layers):
            thick = depth_ref[l] * height[l]
            edge_out[turn, 0, l : l + 1, :] = thick[0:1, :]
            edge_out[turn, 1, l : l + 1, :] = thick[tile_rows - 1 :, :]
            edge_out[turn, 0, layers + l : layers + l + 1, :] = east_mix[l][0:1, :]
            edge_out[turn, 1, layers + l : layers + l + 1, :] = east_mix[l][tile_rows - 1 :, :]
        to_before = copy(edge_out.at[turn, 0], edge_in.at[turn, 0], 2 * turn, before)
        to_after = copy(edge_out.at[turn, 1], edge_in.at[turn, 1], 2 * turn + 1, after)
        to_before.start()
        to_after.start()
        copies += [to_before, to_after]
        if turn == 0:
            spill_copy.wait_recv()
            for l in range(layers):
                number = step * layers + l
                height[l] += jnp.where(first, spill_in[number : number + 1, :], 0.0)
        for l in range(layers):
            thick = depth_ref[l] * height[l]
            north_mix = mixed(north, l)
            out_ref[l] = height[l] + half * (rows_inside(east_mix[l]) + cols(north_mix))
            out_ref[layers + l] = (
                east[l]
                + half * rows_inside(thick)
                - time_step * (coriolis * north[l] + friction * east[l])
            )
            out_ref[2 * layers + l] = (
                north[l]
                + half * cols(thick)
                + time_step * (coriolis * east[l] - friction * north[l])
            )
        to_before.wait_recv()
        to_after.wait_recv()
        if turn == 0:
            depth_copy.wait_recv()
        for l in range(layers):
            below = edge_in[turn, 0, l : l + 1, :]
            if turn == 0:
                number = step * layers + l
                below += depth_in[l : l + 1, :] * spill_ref[number : number + 1, :]
            above = edge_in[turn, 1, l : l + 1, :]
            below_mix = edge_in[turn, 0, layers + l : layers + l + 1, :]
            above_mix = edge_in[turn, 1, layers + l : layers + l + 1, :]
            out_ref[l, 0:1, :] += -half * above_mix
            out_ref[l, tile_rows - 1 :, :] += half * below_mix
            out_ref[layers + l, 0:1, :] += -half * above
            out_ref[layers + l, tile_rows - 1 :, :] += half * below
    for one in copies:
        one.wait_send()


def stencil(adjoint, depth, forcing, spill):
    layers, tile_rows, columns = depth.shape
    planes = forcing.shape[0]
    vmem = pl.BlockSpec(memory_space=pltpu.VMEM)
    return pl.pallas_call(
        stencil_kernel,
        out_shape=jax.ShapeDtypeStruct((3 * layers, tile_rows, columns), jnp.float32),
        in_specs=[vmem] * 4,
        out_specs=vmem,
        scratch_shapes=[
            pltpu.VMEM((STEPS, 2, 2 * layers, columns), jnp.float32),
            pltpu.VMEM((STEPS, 2, 2 * layers, columns), jnp.float32),
            pltpu.VMEM((layers, columns), jnp.float32),
            pltpu.VMEM((layers, columns), jnp.float32),
            pltpu.VMEM((planes, columns), jnp.float32),
            pltpu.SemaphoreType.DMA((2 * STEPS + 2,)),
            pltpu.SemaphoreType.DMA((2 * STEPS + 2,)),
        ],
        compiler_params=pltpu.CompilerParams(
            collective_id=0, has_side_effects=True, vmem_limit_bytes=32 * 1024 * 1024
        ),
        name="stencil",
    )(adjoint, depth, forcing, spill)


def body(
    adjoint_in, layer_depth, obs_cell, obs_plane, obs_owner, innovation, obs_weight, obs_count
):
    tiles = lax.axis_size("space")
    layer_count = layer_depth.shape[0]
    tile_rows = layer_depth.shape[1]
    columns = layer_depth.shape[2]
    obs_rows = obs_cell.shape[1]
    capacity = 5 * obs_rows // (4 * tiles)
    planes = STEPS * layer_count
    windows = lax.axis_size("tm")
    following = lax.ppermute(adjoint_in, "tm", [(i + 1, i) for i in range(windows - 1)])
    lines = obs_rows // LANES
    buffer = route(
        obs_cell.reshape(lines, LANES),
        obs_plane.reshape(lines, LANES),
        obs_owner.reshape(lines, LANES),
        innovation.reshape(lines, LANES),
        obs_weight.reshape(4, lines, LANES),
        obs_count,
        tiles,
        capacity,
        columns,
        tile_rows,
    )
    arrived = lax.all_to_all(buffer, "space", split_axis=0, concat_axis=0, tiled=True)
    forcing, spill = force(arrived, planes, tile_rows, columns)
    adjoint = following[0].reshape(3 * layer_count, tile_rows, columns)
    current = stencil(adjoint, layer_depth, forcing, spill)
    result = adjoint_in[0] - current.reshape(3, layer_count, tile_rows, columns)
    return result[None]


def solution(mesh):
    in_specs = (
        P(("ens", "tm"), None, None, "space", None),
        P(None, "space", None),
        P(("ens", "tm"), "space"),
        P(("ens", "tm"), "space"),
        P(("ens", "tm"), "space", None),
        P(("ens", "tm"), "space"),
        P(None, ("ens", "tm"), "space"),
        P(("ens", "tm"), "space"),
    )
    out_specs = P(("ens", "tm"), None, None, "space", None)
    return jax.shard_map(body, mesh=mesh, in_specs=in_specs, out_specs=out_specs, check_vma=False)
```

```python
import functools

import jax
import jax.numpy as jnp
from jax import lax
from jax.experimental import pallas as pl
from jax.experimental.pallas import tpu as pltpu
from jax.sharding import PartitionSpec as P

STEPS = 4
LANES = 128
WINDOW = 256
FIELDS = 6
GROUP = 4

time_step = 0.4
friction = 0.05
coriolis_mid = 0.3
coriolis_slope = 0.2
coupling = ((1.0, 0.5, 0.25), (0.5, 1.0, 0.5), (0.25, 0.5, 1.0))

NT = (((1,), (1,)), ((), ()))


def spread(row, rows):
    part = jnp.broadcast_to(row, (16, row.shape[1])).astype(jnp.bfloat16)
    return jnp.concatenate([part] * (rows // 16), axis=0)


def one_hot(index_row, rows):
    places = lax.broadcasted_iota(jnp.int32, (rows, index_row.shape[1]), 0)
    return jnp.where(places == index_row, 1.0, 0.0)


def route_kernel(
    tiles,
    capacity,
    columns,
    tile_rows,
    width,
    count_ref,
    cell_hbm,
    plane_hbm,
    owner_hbm,
    innov_hbm,
    weight_hbm,
    adjoint_hbm,
    out_ref,
    following_hbm,
    cell_ref,
    plane_ref,
    owner_ref,
    innov_ref,
    weight_ref,
    key_ref,
    pos_ref,
    piece_ref,
    hit_ref,
    acc_ref,
    slab_ref,
    load_sem,
    send_sem,
    recv_sem,
):
    loads = [
        pltpu.make_async_copy(source, target, load_sem.at[number])
        for number, (source, target) in enumerate(
            [
                (cell_hbm, cell_ref),
                (owner_hbm, owner_ref),
                (plane_hbm, plane_ref),
                (innov_hbm, innov_ref),
                (weight_hbm, weight_ref),
            ]
        )
    ]
    for load in loads:
        load.start()
    me = lax.axis_index("space")
    window = lax.axis_index("tm")
    windows = lax.axis_size("tm")
    half = tiles // 2
    local = lax.rem(me, half)
    my_base = me - local
    other_base = half - my_base
    barrier = pltpu.get_barrier_semaphore()
    for distance in range(1, tiles):
        pl.semaphore_signal(
            barrier,
            inc=1,
            device_id={"space": lax.rem(me + distance, tiles)},
            device_id_type=pl.DeviceIdType.MESH,
        )
    earlier_window = lax.rem(window + windows - 1, windows)
    for distance in range(1, windows):
        pl.semaphore_signal(
            barrier,
            inc=1,
            device_id={"tm": lax.rem(window + distance, windows)},
            device_id_type=pl.DeviceIdType.MESH,
        )
    pl.semaphore_wait(barrier, tiles - 1 + windows - 1)
    follow = pltpu.make_async_remote_copy(
        src_ref=adjoint_hbm,
        dst_ref=following_hbm,
        send_sem=send_sem.at[tiles],
        recv_sem=recv_sem.at[tiles],
        device_id={"tm": earlier_window},
        device_id_type=pl.DeviceIdType.MESH,
    )
    follow.start()
    for load in loads:
        load.wait()
    lines = cell_ref.shape[0]
    buckets = columns // WINDOW
    keys = tiles * buckets
    slot_rows = tiles * capacity // width
    place = lax.broadcasted_iota(jnp.int32, (lines, LANES), 0) * LANES + lax.broadcasted_iota(
        jnp.int32, (lines, LANES), 1
    )
    live = place < count_ref[0, 0]
    cell = cell_ref[...]
    column = jnp.bitwise_and(cell, columns - 1)
    row = jnp.right_shift(cell, columns.bit_length() - 1)
    bucket = jnp.right_shift(column, WINDOW.bit_length() - 1)
    key_ref[...] = jnp.where(live, owner_ref[...] * buckets + bucket, keys)
    piece_ref[0] = (plane_ref[...] * tile_rows + row + 1).astype(jnp.float32)
    piece_ref[1] = (bucket * WINDOW).astype(jnp.float32)
    piece_ref[2] = jnp.bitwise_and(column, WINDOW - 1).astype(jnp.float32)
    innovation = innov_ref[...]
    for corner in range(4):
        value = weight_ref[corner] * innovation
        high = value.astype(jnp.bfloat16).astype(jnp.float32)
        piece_ref[3 + 2 * corner] = high
        piece_ref[4 + 2 * corner] = value - high

    def count_step(line, total):
        for extra in range(8):
            total += one_hot(key_ref[pl.ds(line * 8 + extra, 1), :], keys)
        return total

    total = lax.fori_loop(0, lines // 8, count_step, jnp.zeros((keys, LANES), jnp.float32))
    mine = lax.broadcasted_iota(jnp.int32, (keys, keys), 0)
    other = lax.broadcasted_iota(jnp.int32, (keys, keys), 1)
    shift = buckets.bit_length() - 1
    same_owner = jnp.right_shift(mine, shift) == jnp.right_shift(other, shift)
    before = jnp.where(same_owner & (other < mine), 1.0, 0.0).astype(jnp.bfloat16)
    ahead = jnp.dot(before, total.astype(jnp.bfloat16), preferred_element_type=jnp.float32)
    owner_of = jnp.right_shift(lax.broadcasted_iota(jnp.int32, (keys, 1), 0), shift)
    base = jnp.sum(ahead, axis=1, keepdims=True) + (owner_of * capacity).astype(jnp.float32)
    triangle = jnp.where(
        lax.broadcasted_iota(jnp.int32, (256, 256), 0)
        < lax.broadcasted_iota(jnp.int32, (256, 256), 1),
        1.0,
        0.0,
    ).astype(jnp.bfloat16)

    def rank_step(step, base):
        for extra in range(4):
            line = step * 8 + extra * 2
            key = jnp.concatenate(
                [key_ref[pl.ds(line, 1), :], key_ref[pl.ds(line + 1, 1), :]], axis=1
            )
            hits = one_hot(key, keys)
            earlier = jnp.dot(
                hits.astype(jnp.bfloat16), triangle, preferred_element_type=jnp.float32
            )
            position = jnp.sum(hits * (earlier + base), axis=0, keepdims=True).astype(jnp.int32)
            position = jnp.where(key < keys, position, -1)
            pos_ref[pl.ds(line, 1), :] = position[:, :LANES]
            pos_ref[pl.ds(line + 1, 1), :] = position[:, LANES:]
            base += jnp.sum(hits, axis=1, keepdims=True)
        return base

    lax.fori_loop(0, lines // 8, rank_step, base)
    log_width = width.bit_length() - 1
    half_rows = slot_rows // 2
    part_rows = (half_rows + 15) // 16 * 16
    per_owner = capacity // width
    per_half = tiles // 2
    span = range(8)

    def move_half(first_row, fresh):
        acc_ref[...] = jnp.zeros_like(acc_ref)

        def move_step(step, carry):
            parts, lefts = [], []
            for extra in span:
                position = pos_ref[pl.ds(step * 8 + extra, 1), :]
                slot = jnp.right_shift(position, log_width) - first_row
                slots = one_hot(slot, part_rows).astype(jnp.bfloat16)
                pieces = [
                    slots * spread(piece_ref[piece, pl.ds(step * 8 + extra, 1), :], part_rows)
                    for piece in range(11)
                ]
                parts.append(jnp.concatenate(pieces, axis=0))
                if fresh:
                    lane = jnp.bitwise_and(position, width - 1)
                    lefts.append(one_hot(lane, width).astype(jnp.bfloat16))
            if fresh:
                lane_hits = jnp.concatenate(lefts, axis=1)
                hit_ref[step] = lane_hits
            else:
                lane_hits = hit_ref[step]
            acc_ref[...] += lax.dot_general(
                jnp.concatenate(parts, axis=1), lane_hits, NT, preferred_element_type=jnp.float32
            )
            return carry

        lax.fori_loop(0, lines // 8, move_step, 0)
        for owner in range(per_half):
            for field in range(FIELDS):

                def piece_rows(piece):
                    first = piece * part_rows + owner * per_owner
                    return acc_ref[first : first + per_owner, :]

                value = piece_rows(0)
                if field > 0:
                    value = piece_rows(2 * field - 1) + piece_rows(2 * field)
                target = slice(field * per_owner, (field + 1) * per_owner)
                slab_ref[0 if fresh else 1, owner, target, :] = value

    def exchange(base, group, number):
        to_local = lax.rem(local + number, half)
        from_tile = base + lax.rem(local + half - number, half)

        def copy(slot):
            return pltpu.make_async_remote_copy(
                src_ref=slab_ref.at[group, to_local],
                dst_ref=out_ref.at[slot],
                send_sem=send_sem.at[group * half + number],
                recv_sem=recv_sem.at[group * half + number],
                device_id={"space": base + to_local},
                device_id_type=pl.DeviceIdType.MESH,
            )

        return copy(me), copy(from_tile)

    pairs = []
    move_half(other_base * per_owner, True)
    for number in range(half):
        pairs.append(exchange(other_base, 0, number))
        pairs[-1][0].start()
    move_half(my_base * per_owner, False)
    for number in range(1, half):
        pairs.append(exchange(my_base, 1, number))
        pairs[-1][0].start()
    out_ref[me] = slab_ref[1, local]
    for sent, got in pairs:
        got.wait_recv()
    follow.wait_recv()
    for sent, got in pairs:
        sent.wait_send()
    follow.wait_send()


def route(
    cell, plane, owner, innov, weights, count, adjoint, tiles, capacity, columns, tile_rows
):
    lines = cell.shape[0]
    width = 256 if capacity % 256 == 0 else LANES
    half_rows = tiles * capacity // width // 2
    part_rows = (half_rows + 15) // 16 * 16
    depth = FIELDS * (capacity // width)
    vmem = pl.BlockSpec(memory_space=pltpu.VMEM)
    anywhere = pl.BlockSpec(memory_space=pl.ANY)
    whole = pltpu.VMEM((lines, LANES), jnp.int32)
    return pl.pallas_call(
        functools.partial(route_kernel, tiles, capacity, columns, tile_rows, width),
        out_shape=(
            jax.ShapeDtypeStruct((tiles, depth, width), jnp.float32),
            jax.ShapeDtypeStruct(adjoint.shape, adjoint.dtype),
        ),
        in_specs=[pl.BlockSpec(memory_space=pltpu.SMEM)] + [anywhere] * 6,
        out_specs=(vmem, anywhere),
        scratch_shapes=[
            whole,
            whole,
            whole,
            pltpu.VMEM((lines, LANES), jnp.float32),
            pltpu.VMEM((4, lines, LANES), jnp.float32),
            whole,
            whole,
            pltpu.VMEM((11, lines, LANES), jnp.float32),
            pltpu.VMEM((lines // 8, width, 8 * LANES), jnp.bfloat16),
            pltpu.VMEM((11 * part_rows, width), jnp.float32),
            pltpu.VMEM((2, tiles // 2, depth, width), jnp.float32),
            pltpu.SemaphoreType.DMA((5,)),
            pltpu.SemaphoreType.DMA((tiles + 1,)),
            pltpu.SemaphoreType.DMA((tiles + 1,)),
        ],
        compiler_params=pltpu.CompilerParams(
            collective_id=1, has_side_effects=True, vmem_limit_bytes=48 * 1024 * 1024
        ),
        name="route",
    )(count, cell, plane, owner, innov, weights, adjoint)


def force_kernel(
    planes, tile_rows, columns, low_ref, high_ref, in_ref, out_ref, spill_ref, acc_ref, item_ref
):
    tiles, depth, width = in_ref.shape
    per_tile = depth // FIELDS
    cells = planes * tile_rows
    windows = columns // WINDOW
    acc_ref[...] = jnp.zeros_like(acc_ref)

    def list_source(source, count):
        def list_block(block, count):
            number = source * per_tile + block

            def list_window(window, count):
                item_ref[0, count] = source
                item_ref[1, count] = block
                item_ref[2, count] = window
                item_ref[3, count] = window
                return count + 1

            return lax.fori_loop(low_ref[number], high_ref[number] + 1, list_window, count)

        return lax.fori_loop(0, per_tile, list_block, count)

    count = lax.fori_loop(0, tiles, list_source, 0)
    for extra in range(GROUP):
        item_ref[0, count + extra] = 0
        item_ref[1, count + extra] = 0
        item_ref[2, count + extra] = windows
        item_ref[3, count + extra] = 0

    def product(item):
        source, block = item_ref[0, item], item_ref[1, item]

        def field(number):
            return in_ref[source, pl.ds(number * per_tile + block, 1), :]

        line = field(0).astype(jnp.int32) - 1
        column = field(1).astype(jnp.int32)
        line_hits = one_hot(line, cells).astype(jnp.bfloat16)
        highs, lows = [], []
        for corner in range(4):
            value = field(2 + corner)
            high = value.astype(jnp.bfloat16).astype(jnp.float32)
            highs.append(line_hits * spread(high, cells))
            lows.append(line_hits * spread(value - high, cells))
        left = jnp.concatenate(
            [jnp.concatenate(highs, axis=0), jnp.concatenate(lows, axis=0)], axis=1
        )
        hits = one_hot(column - item_ref[2, item] * WINDOW, WINDOW).astype(jnp.bfloat16)
        right = jnp.concatenate([hits, hits], axis=1)
        return lax.dot_general(left, right, NT, preferred_element_type=jnp.float32)

    def group_step(group, carry):
        found = [product(group * GROUP + extra) for extra in range(GROUP)]
        for extra in range(GROUP):
            acc_ref[item_ref[3, group * GROUP + extra]] += found[extra]
        return carry

    lax.fori_loop(0, (count + GROUP - 1) // GROUP, group_step, 0)
    row = lax.broadcasted_iota(jnp.int32, (tile_rows, columns), 0)
    for plane in range(planes):

        def gathered(corner):
            first = corner * cells + plane * tile_rows
            return jnp.concatenate(
                [acc_ref[w, first : first + tile_rows, :] for w in range(columns // WINDOW)],
                axis=1,
            )

        here = gathered(0) + pltpu.roll(gathered(1), 1, axis=1)
        below = gathered(2) + pltpu.roll(gathered(3), 1, axis=1)
        below = pltpu.roll(below, 1, axis=0)
        out_ref[plane] = here + jnp.where(row > 0, below, 0.0)
        spill_ref[plane : plane + 1, :] = below[0:1, :]


def force(arrived, planes, tile_rows, columns):
    tiles, depth, width = arrived.shape
    per_tile = depth // FIELDS
    line = arrived[:, :per_tile]
    column = arrived[:, per_tile : 2 * per_tile]
    low = jnp.min(jnp.where(line > 0, column, float(columns)), axis=2).reshape(tiles * per_tile)
    high = jnp.max(jnp.where(line > 0, column, -1.0), axis=2).reshape(tiles * per_tile)
    low = jnp.floor(low / WINDOW).astype(jnp.int32)
    high = jnp.floor(high / WINDOW).astype(jnp.int32)
    vmem = pl.BlockSpec(memory_space=pltpu.VMEM)
    smem = pl.BlockSpec(memory_space=pltpu.SMEM)
    shape = jax.ShapeDtypeStruct((planes, tile_rows, columns), jnp.float32)
    return pl.pallas_call(
        functools.partial(force_kernel, planes, tile_rows, columns),
        out_shape=(shape, jax.ShapeDtypeStruct((planes, columns), jnp.float32)),
        in_specs=[smem, smem, vmem],
        out_specs=(vmem, vmem),
        scratch_shapes=[
            pltpu.VMEM((columns // WINDOW, 4 * planes * tile_rows, WINDOW), jnp.float32),
            pltpu.SMEM((4, tiles * (per_tile * 2 + 2 * columns // WINDOW) + GROUP), jnp.int32),
        ],
        compiler_params=pltpu.CompilerParams(vmem_limit_bytes=48 * 1024 * 1024),
        name="force",
    )(low, high, arrived)


def stencil_kernel(
    adjoint_ref,
    depth_ref,
    forcing_ref,
    spill_ref,
    out_ref,
    edge_out,
    edge_in,
    depth_out,
    depth_in,
    spill_in,
    send_sem,
    recv_sem,
):
    layers, tile_rows, columns = depth_ref.shape
    tiles = lax.axis_size("space")
    me = lax.axis_index("space")
    after = lax.rem(me + 1, tiles)
    before = lax.rem(me + tiles - 1, tiles)
    barrier = pltpu.get_barrier_semaphore()
    for neighbour in (before, after):
        pl.semaphore_signal(
            barrier,
            inc=1,
            device_id={"space": neighbour},
            device_id_type=pl.DeviceIdType.MESH,
        )
    pl.semaphore_wait(barrier, 2)

    def copy(source, target, number, neighbour):
        return pltpu.make_async_remote_copy(
            src_ref=source,
            dst_ref=target,
            send_sem=send_sem.at[number],
            recv_sem=recv_sem.at[number],
            device_id={"space": neighbour},
            device_id_type=pl.DeviceIdType.MESH,
        )

    spill_copy = copy(spill_ref, spill_in, 2 * STEPS, after)
    depth_copy = copy(depth_out, depth_in, 2 * STEPS + 1, before)
    spill_copy.start()
    for layer in range(layers):
        depth_out[layer : layer + 1, :] = depth_ref[layer, 0:1, :]
    depth_copy.start()

    row = lax.broadcasted_iota(jnp.int32, (tile_rows, columns), 0)
    first, last = row == 0, row == tile_rows - 1
    place = lax.broadcasted_iota(jnp.int32, (tile_rows, columns), 1).astype(jnp.float32)
    coriolis = coriolis_mid + coriolis_slope * (place / columns - 0.5)
    half = 0.5 * time_step

    def rows_inside(field):
        ahead = jnp.where(last, 0.0, pltpu.roll(field, tile_rows - 1, axis=0))
        behind = jnp.where(first, 0.0, pltpu.roll(field, 1, axis=0))
        return ahead - behind

    def cols(field):
        return pltpu.roll(field, columns - 1, axis=1) - pltpu.roll(field, 1, axis=1)

    def mixed(fields, m):
        return sum(coupling[l][m] * fields[l] for l in range(3))

    goes_on = jnp.where(lax.axis_index("tm") == lax.axis_size("tm") - 1, 0, 1)

    def started(number):
        return jnp.where(goes_on > 0, adjoint_ref[number], 0.0)

    copies = [spill_copy, depth_copy]
    for turn in range(STEPS):
        step = STEPS - 1 - turn
        state = started if turn == 0 else out_ref.__getitem__
        height = [state(l) + forcing_ref[step * layers + l] for l in range(layers)]
        if turn > 0:
            for l in range(layers):
                number = step * layers + l
                height[l] += jnp.where(first, spill_in[number : number + 1, :], 0.0)
        east = [state(layers + l) for l in range(layers)]
        north = [state(2 * layers + l) for l in range(layers)]
        east_mix = [mixed(east, m) for m in range(layers)]
        for l in range(layers):
            thick = depth_ref[l] * height[l]
            edge_out[turn, 0, l : l + 1, :] = thick[0:1, :]
            edge_out[turn, 1, l : l + 1, :] = thick[tile_rows - 1 :, :]
            edge_out[turn, 0, layers + l : layers + l + 1, :] = east_mix[l][0:1, :]
            edge_out[turn, 1, layers + l : layers + l + 1, :] = east_mix[l][tile_rows - 1 :, :]
        to_before = copy(edge_out.at[turn, 0], edge_in.at[turn, 0], 2 * turn, before)
        to_after = copy(edge_out.at[turn, 1], edge_in.at[turn, 1], 2 * turn + 1, after)
        to_before.start()
        to_after.start()
        copies += [to_before, to_after]
        if turn == 0:
            spill_copy.wait_recv()
            for l in range(layers):
                number = step * layers + l
                height[l] += jnp.where(first, spill_in[number : number + 1, :], 0.0)
        for l in range(layers):
            thick = depth_ref[l] * height[l]
            north_mix = mixed(north, l)
            out_ref[l] = height[l] + half * (rows_inside(east_mix[l]) + cols(north_mix))
            out_ref[layers + l] = (
                east[l]
                + half * rows_inside(thick)
                - time_step * (coriolis * north[l] + friction * east[l])
            )
            out_ref[2 * layers + l] = (
                north[l]
                + half * cols(thick)
                + time_step * (coriolis * east[l] - friction * north[l])
            )
        to_before.wait_recv()
        to_after.wait_recv()
        if turn == 0:
            depth_copy.wait_recv()
        for l in range(layers):
            below = edge_in[turn, 0, l : l + 1, :]
            if turn == 0:
                number = step * layers + l
                below += depth_in[l : l + 1, :] * spill_ref[number : number + 1, :]
            above = edge_in[turn, 1, l : l + 1, :]
            below_mix = edge_in[turn, 0, layers + l : layers + l + 1, :]
            above_mix = edge_in[turn, 1, layers + l : layers + l + 1, :]
            out_ref[l, 0:1, :] += -half * above_mix
            out_ref[l, tile_rows - 1 :, :] += half * below_mix
            out_ref[layers + l, 0:1, :] += -half * above
            out_ref[layers + l, tile_rows - 1 :, :] += half * below
    for one in copies:
        one.wait_send()


def stencil(adjoint, depth, forcing, spill):
    layers, tile_rows, columns = depth.shape
    planes = forcing.shape[0]
    vmem = pl.BlockSpec(memory_space=pltpu.VMEM)
    return pl.pallas_call(
        stencil_kernel,
        out_shape=jax.ShapeDtypeStruct((3 * layers, tile_rows, columns), jnp.float32),
        in_specs=[vmem] * 4,
        out_specs=vmem,
        scratch_shapes=[
            pltpu.VMEM((STEPS, 2, 2 * layers, columns), jnp.float32),
            pltpu.VMEM((STEPS, 2, 2 * layers, columns), jnp.float32),
            pltpu.VMEM((layers, columns), jnp.float32),
            pltpu.VMEM((layers, columns), jnp.float32),
            pltpu.VMEM((planes, columns), jnp.float32),
            pltpu.SemaphoreType.DMA((2 * STEPS + 2,)),
            pltpu.SemaphoreType.DMA((2 * STEPS + 2,)),
        ],
        compiler_params=pltpu.CompilerParams(
            collective_id=0, has_side_effects=True, vmem_limit_bytes=32 * 1024 * 1024
        ),
        name="stencil",
    )(adjoint, depth, forcing, spill)


def body(
    adjoint_in, layer_depth, obs_cell, obs_plane, obs_owner, innovation, obs_weight, obs_count
):
    tiles = lax.axis_size("space")
    layer_count = layer_depth.shape[0]
    tile_rows = layer_depth.shape[1]
    columns = layer_depth.shape[2]
    obs_rows = obs_cell.shape[1]
    capacity = 5 * obs_rows // (4 * tiles)
    planes = STEPS * layer_count
    lines = obs_rows // LANES
    adjoint = adjoint_in[0].reshape(3 * layer_count, tile_rows, columns)
    arrived, following = route(
        obs_cell.reshape(lines, LANES),
        obs_plane.reshape(lines, LANES),
        obs_owner.reshape(lines, LANES),
        innovation.reshape(lines, LANES),
        obs_weight.reshape(4, lines, LANES),
        obs_count,
        adjoint,
        tiles,
        capacity,
        columns,
        tile_rows,
    )
    forcing, spill = force(arrived, planes, tile_rows, columns)
    current = stencil(following, layer_depth, forcing, spill)
    result = adjoint_in[0] - current.reshape(3, layer_count, tile_rows, columns)
    return result[None]


def solution(mesh):
    in_specs = (
        P(("ens", "tm"), None, None, "space", None),
        P(None, "space", None),
        P(("ens", "tm"), "space"),
        P(("ens", "tm"), "space"),
        P(("ens", "tm"), "space", None),
        P(("ens", "tm"), "space"),
        P(None, ("ens", "tm"), "space"),
        P(("ens", "tm"), "space"),
    )
    out_specs = P(("ens", "tm"), None, None, "space", None)
    return jax.shard_map(body, mesh=mesh, in_specs=in_specs, out_specs=out_specs, check_vma=False)
```

```python
import functools

import jax
import jax.numpy as jnp
from jax import lax
from jax.experimental import pallas as pl
from jax.experimental.pallas import tpu as pltpu
from jax.sharding import PartitionSpec as P

STEPS = 4
LANES = 128
WINDOW = 256
FIELDS = 6
GROUP = 8

time_step = 0.4
friction = 0.05
coriolis_mid = 0.3
coriolis_slope = 0.2
coupling = ((1.0, 0.5, 0.25), (0.5, 1.0, 0.5), (0.25, 0.5, 1.0))

NT = (((1,), (1,)), ((), ()))


def spread(row, rows):
    part = jnp.broadcast_to(row, (16, row.shape[1])).astype(jnp.bfloat16)
    return jnp.concatenate([part] * (rows // 16), axis=0)


def one_hot(index_row, rows):
    places = lax.broadcasted_iota(jnp.int32, (rows, index_row.shape[1]), 0)
    return jnp.where(places == index_row, 1.0, 0.0)


def one_hot_16(index_row, rows):
    places = lax.broadcasted_iota(jnp.int32, (rows, index_row.shape[1]), 0)
    places = places.astype(jnp.float32).astype(jnp.bfloat16)
    same = places == spread(index_row.astype(jnp.float32), rows)
    return jnp.where(same, jnp.bfloat16(1), jnp.bfloat16(0))


def route_kernel(
    tiles,
    capacity,
    columns,
    tile_rows,
    width,
    count_ref,
    cell_hbm,
    plane_hbm,
    owner_hbm,
    innov_hbm,
    weight_hbm,
    adjoint_hbm,
    out_ref,
    following_hbm,
    cell_ref,
    plane_ref,
    owner_ref,
    innov_ref,
    weight_ref,
    key_ref,
    pos_ref,
    piece_ref,
    hit_ref,
    acc_ref,
    slab_ref,
    load_sem,
    send_sem,
    recv_sem,
):
    loads = [
        pltpu.make_async_copy(source, target, load_sem.at[number])
        for number, (source, target) in enumerate(
            [
                (cell_hbm, cell_ref),
                (owner_hbm, owner_ref),
                (plane_hbm, plane_ref),
                (innov_hbm, innov_ref),
                (weight_hbm, weight_ref),
            ]
        )
    ]
    for load in loads:
        load.start()
    me = lax.axis_index("space")
    window = lax.axis_index("tm")
    windows = lax.axis_size("tm")
    half = tiles // 2
    local = lax.rem(me, half)
    my_base = me - local
    other_base = half - my_base
    barrier = pltpu.get_barrier_semaphore()
    for distance in range(1, tiles):
        pl.semaphore_signal(
            barrier,
            inc=1,
            device_id={"space": lax.rem(me + distance, tiles)},
            device_id_type=pl.DeviceIdType.MESH,
        )
    earlier_window = lax.rem(window + windows - 1, windows)
    for distance in range(1, windows):
        pl.semaphore_signal(
            barrier,
            inc=1,
            device_id={"tm": lax.rem(window + distance, windows)},
            device_id_type=pl.DeviceIdType.MESH,
        )
    pl.semaphore_wait(barrier, tiles - 1 + windows - 1)
    follow = pltpu.make_async_remote_copy(
        src_ref=adjoint_hbm,
        dst_ref=following_hbm,
        send_sem=send_sem.at[tiles],
        recv_sem=recv_sem.at[tiles],
        device_id={"tm": earlier_window},
        device_id_type=pl.DeviceIdType.MESH,
    )
    follow.start()
    for load in loads:
        load.wait()
    lines = cell_ref.shape[0]
    buckets = columns // WINDOW
    keys = tiles * buckets
    slot_rows = tiles * capacity // width
    place = lax.broadcasted_iota(jnp.int32, (lines, LANES), 0) * LANES + lax.broadcasted_iota(
        jnp.int32, (lines, LANES), 1
    )
    live = place < count_ref[0, 0]
    cell = cell_ref[...]
    column = jnp.bitwise_and(cell, columns - 1)
    row = jnp.right_shift(cell, columns.bit_length() - 1)
    bucket = jnp.right_shift(column, WINDOW.bit_length() - 1)
    key_ref[...] = jnp.where(live, owner_ref[...] * buckets + bucket, keys)
    piece_ref[0] = (plane_ref[...] * tile_rows + row + 1).astype(jnp.float32)
    piece_ref[1] = (bucket * WINDOW).astype(jnp.float32)
    piece_ref[2] = jnp.bitwise_and(column, WINDOW - 1).astype(jnp.float32)
    innovation = innov_ref[...]
    for corner in range(4):
        value = weight_ref[corner] * innovation
        high = value.astype(jnp.bfloat16).astype(jnp.float32)
        piece_ref[3 + 2 * corner] = high
        piece_ref[4 + 2 * corner] = value - high

    def count_step(line, total):
        for extra in range(8):
            total += one_hot(key_ref[pl.ds(line * 8 + extra, 1), :], keys)
        return total

    total = lax.fori_loop(0, lines // 8, count_step, jnp.zeros((keys, LANES), jnp.float32))
    mine = lax.broadcasted_iota(jnp.int32, (keys, keys), 0)
    other = lax.broadcasted_iota(jnp.int32, (keys, keys), 1)
    shift = buckets.bit_length() - 1
    same_owner = jnp.right_shift(mine, shift) == jnp.right_shift(other, shift)
    before = jnp.where(same_owner & (other < mine), 1.0, 0.0).astype(jnp.bfloat16)
    ahead = jnp.dot(before, total.astype(jnp.bfloat16), preferred_element_type=jnp.float32)
    owner_of = jnp.right_shift(lax.broadcasted_iota(jnp.int32, (keys, 1), 0), shift)
    base = jnp.sum(ahead, axis=1, keepdims=True) + (owner_of * capacity).astype(jnp.float32)
    triangle = jnp.where(
        lax.broadcasted_iota(jnp.int32, (256, 256), 0)
        < lax.broadcasted_iota(jnp.int32, (256, 256), 1),
        1.0,
        0.0,
    ).astype(jnp.bfloat16)

    def rank_step(step, base):
        for extra in range(4):
            line = step * 8 + extra * 2
            key = jnp.concatenate(
                [key_ref[pl.ds(line, 1), :], key_ref[pl.ds(line + 1, 1), :]], axis=1
            )
            hits = one_hot(key, keys)
            earlier = jnp.dot(
                hits.astype(jnp.bfloat16), triangle, preferred_element_type=jnp.float32
            )
            position = jnp.sum(hits * (earlier + base), axis=0, keepdims=True).astype(jnp.int32)
            position = jnp.where(key < keys, position, -1)
            pos_ref[pl.ds(line, 1), :] = position[:, :LANES]
            pos_ref[pl.ds(line + 1, 1), :] = position[:, LANES:]
            base += jnp.sum(hits, axis=1, keepdims=True)
        return base

    lax.fori_loop(0, lines // 8, rank_step, base)
    log_width = width.bit_length() - 1
    half_rows = slot_rows // 2
    part_rows = (half_rows + 15) // 16 * 16
    per_owner = capacity // width
    per_half = tiles // 2
    span = range(8)

    def move_half(first_row, fresh):
        acc_ref[...] = jnp.zeros_like(acc_ref)

        def move_step(step, carry):
            parts, lefts = [], []
            for extra in span:
                position = pos_ref[pl.ds(step * 8 + extra, 1), :]
                slot = jnp.right_shift(position, log_width) - first_row
                slots = one_hot_16(slot, part_rows)
                pieces = [
                    slots * spread(piece_ref[piece, pl.ds(step * 8 + extra, 1), :], part_rows)
                    for piece in range(11)
                ]
                parts.append(jnp.concatenate(pieces, axis=0))
                if fresh:
                    lane = jnp.bitwise_and(position, width - 1)
                    lefts.append(one_hot_16(lane, width))
            if fresh:
                lane_hits = jnp.concatenate(lefts, axis=1)
                hit_ref[step] = lane_hits
            else:
                lane_hits = hit_ref[step]
            acc_ref[...] += lax.dot_general(
                jnp.concatenate(parts, axis=1), lane_hits, NT, preferred_element_type=jnp.float32
            )
            return carry

        lax.fori_loop(0, lines // 8, move_step, 0)
        for owner in range(per_half):
            for field in range(FIELDS):

                def piece_rows(piece):
                    first = piece * part_rows + owner * per_owner
                    return acc_ref[first : first + per_owner, :]

                value = piece_rows(0)
                if field > 0:
                    value = piece_rows(2 * field - 1) + piece_rows(2 * field)
                target = slice(field * per_owner, (field + 1) * per_owner)
                slab_ref[0 if fresh else 1, owner, target, :] = value

    def exchange(base, group, number):
        to_local = lax.rem(local + number, half)
        from_tile = base + lax.rem(local + half - number, half)

        def copy(slot):
            return pltpu.make_async_remote_copy(
                src_ref=slab_ref.at[group, to_local],
                dst_ref=out_ref.at[slot],
                send_sem=send_sem.at[group * half + number],
                recv_sem=recv_sem.at[group * half + number],
                device_id={"space": base + to_local},
                device_id_type=pl.DeviceIdType.MESH,
            )

        return copy(me), copy(from_tile)

    pairs = []
    move_half(other_base * per_owner, True)
    for number in range(half):
        pairs.append(exchange(other_base, 0, number))
        pairs[-1][0].start()
    move_half(my_base * per_owner, False)
    for number in range(1, half):
        pairs.append(exchange(my_base, 1, number))
        pairs[-1][0].start()
    out_ref[me] = slab_ref[1, local]
    for sent, got in pairs:
        got.wait_recv()
    follow.wait_recv()
    for sent, got in pairs:
        sent.wait_send()
    follow.wait_send()


def route(
    cell, plane, owner, innov, weights, count, adjoint, tiles, capacity, columns, tile_rows
):
    lines = cell.shape[0]
    width = 256 if capacity % 256 == 0 else LANES
    half_rows = tiles * capacity // width // 2
    part_rows = (half_rows + 15) // 16 * 16
    depth = FIELDS * (capacity // width)
    vmem = pl.BlockSpec(memory_space=pltpu.VMEM)
    anywhere = pl.BlockSpec(memory_space=pltpu.HBM)
    whole = pltpu.VMEM((lines, LANES), jnp.int32)
    return pl.pallas_call(
        functools.partial(route_kernel, tiles, capacity, columns, tile_rows, width),
        out_shape=(
            jax.ShapeDtypeStruct((tiles, depth, width), jnp.float32),
            jax.ShapeDtypeStruct(adjoint.shape, adjoint.dtype),
        ),
        in_specs=[pl.BlockSpec(memory_space=pltpu.SMEM)] + [anywhere] * 6,
        out_specs=(vmem, anywhere),
        scratch_shapes=[
            whole,
            whole,
            whole,
            pltpu.VMEM((lines, LANES), jnp.float32),
            pltpu.VMEM((4, lines, LANES), jnp.float32),
            whole,
            whole,
            pltpu.VMEM((11, lines, LANES), jnp.float32),
            pltpu.VMEM((lines // 8, width, 8 * LANES), jnp.bfloat16),
            pltpu.VMEM((11 * part_rows, width), jnp.float32),
            pltpu.VMEM((2, tiles // 2, depth, width), jnp.float32),
            pltpu.SemaphoreType.DMA((5,)),
            pltpu.SemaphoreType.DMA((tiles + 1,)),
            pltpu.SemaphoreType.DMA((tiles + 1,)),
        ],
        compiler_params=pltpu.CompilerParams(
            collective_id=1, has_side_effects=True, vmem_limit_bytes=48 * 1024 * 1024
        ),
        name="route",
    )(count, cell, plane, owner, innov, weights, adjoint)


def force_kernel(
    planes, tile_rows, columns, low_ref, high_ref, in_ref, out_ref, spill_ref, acc_ref, item_ref
):
    tiles, depth, width = in_ref.shape
    per_tile = depth // FIELDS
    cells = planes * tile_rows
    windows = columns // WINDOW
    acc_ref[...] = jnp.zeros_like(acc_ref)

    def list_source(source, count):
        def list_block(block, count):
            number = source * per_tile + block

            def list_window(window, count):
                item_ref[0, count] = source
                item_ref[1, count] = block
                item_ref[2, count] = window
                item_ref[3, count] = window
                return count + 1

            return lax.fori_loop(low_ref[number], high_ref[number] + 1, list_window, count)

        return lax.fori_loop(0, per_tile, list_block, count)

    count = lax.fori_loop(0, tiles, list_source, 0)
    for extra in range(GROUP):
        item_ref[0, count + extra] = 0
        item_ref[1, count + extra] = 0
        item_ref[2, count + extra] = windows
        item_ref[3, count + extra] = 0

    def product(item):
        source, block = item_ref[0, item], item_ref[1, item]

        def field(number):
            return in_ref[source, pl.ds(number * per_tile + block, 1), :]

        line = field(0).astype(jnp.int32) - 1
        column = field(1).astype(jnp.int32)
        line_hits = one_hot_16(line, cells)
        highs, lows = [], []
        for corner in range(4):
            value = field(2 + corner)
            high = value.astype(jnp.bfloat16).astype(jnp.float32)
            highs.append(line_hits * spread(high, cells))
            lows.append(line_hits * spread(value - high, cells))
        left = jnp.concatenate(
            [jnp.concatenate(highs, axis=0), jnp.concatenate(lows, axis=0)], axis=1
        )
        hits = one_hot_16(column - item_ref[2, item] * WINDOW, WINDOW)
        right = jnp.concatenate([hits, hits], axis=1)
        return lax.dot_general(left, right, NT, preferred_element_type=jnp.float32)

    def group_step(group, carry):
        found = [product(group * GROUP + extra) for extra in range(GROUP)]
        for extra in range(GROUP):
            acc_ref[item_ref[3, group * GROUP + extra]] += found[extra]
        return carry

    lax.fori_loop(0, (count + GROUP - 1) // GROUP, group_step, 0)
    row = lax.broadcasted_iota(jnp.int32, (tile_rows, columns), 0)
    for plane in range(planes):

        def gathered(corner):
            first = corner * cells + plane * tile_rows
            return jnp.concatenate(
                [acc_ref[w, first : first + tile_rows, :] for w in range(columns // WINDOW)],
                axis=1,
            )

        here = gathered(0) + pltpu.roll(gathered(1), 1, axis=1)
        below = gathered(2) + pltpu.roll(gathered(3), 1, axis=1)
        below = pltpu.roll(below, 1, axis=0)
        out_ref[plane] = here + jnp.where(row > 0, below, 0.0)
        spill_ref[plane : plane + 1, :] = below[0:1, :]


def force(arrived, planes, tile_rows, columns):
    tiles, depth, width = arrived.shape
    per_tile = depth // FIELDS
    line = arrived[:, :per_tile]
    column = arrived[:, per_tile : 2 * per_tile]
    low = jnp.min(jnp.where(line > 0, column, float(columns)), axis=2).reshape(tiles * per_tile)
    high = jnp.max(jnp.where(line > 0, column, -1.0), axis=2).reshape(tiles * per_tile)
    low = jnp.floor(low / WINDOW).astype(jnp.int32)
    high = jnp.floor(high / WINDOW).astype(jnp.int32)
    vmem = pl.BlockSpec(memory_space=pltpu.VMEM)
    smem = pl.BlockSpec(memory_space=pltpu.SMEM)
    shape = jax.ShapeDtypeStruct((planes, tile_rows, columns), jnp.float32)
    return pl.pallas_call(
        functools.partial(force_kernel, planes, tile_rows, columns),
        out_shape=(shape, jax.ShapeDtypeStruct((planes, columns), jnp.float32)),
        in_specs=[smem, smem, vmem],
        out_specs=(vmem, vmem),
        scratch_shapes=[
            pltpu.VMEM((columns // WINDOW, 4 * planes * tile_rows, WINDOW), jnp.float32),
            pltpu.SMEM((4, tiles * (per_tile * 2 + 2 * columns // WINDOW) + GROUP), jnp.int32),
        ],
        compiler_params=pltpu.CompilerParams(vmem_limit_bytes=48 * 1024 * 1024),
        name="force",
    )(low, high, arrived)


def stencil_kernel(
    adjoint_ref,
    depth_ref,
    forcing_ref,
    spill_ref,
    out_ref,
    edge_out,
    edge_in,
    depth_out,
    depth_in,
    spill_in,
    send_sem,
    recv_sem,
):
    layers, tile_rows, columns = depth_ref.shape
    tiles = lax.axis_size("space")
    me = lax.axis_index("space")
    after = lax.rem(me + 1, tiles)
    before = lax.rem(me + tiles - 1, tiles)
    barrier = pltpu.get_barrier_semaphore()
    for neighbour in (before, after):
        pl.semaphore_signal(
            barrier,
            inc=1,
            device_id={"space": neighbour},
            device_id_type=pl.DeviceIdType.MESH,
        )
    pl.semaphore_wait(barrier, 2)

    def copy(source, target, number, neighbour):
        return pltpu.make_async_remote_copy(
            src_ref=source,
            dst_ref=target,
            send_sem=send_sem.at[number],
            recv_sem=recv_sem.at[number],
            device_id={"space": neighbour},
            device_id_type=pl.DeviceIdType.MESH,
        )

    spill_copy = copy(spill_ref, spill_in, 2 * STEPS, after)
    depth_copy = copy(depth_out, depth_in, 2 * STEPS + 1, before)
    spill_copy.start()
    for layer in range(layers):
        depth_out[layer : layer + 1, :] = depth_ref[layer, 0:1, :]
    depth_copy.start()

    row = lax.broadcasted_iota(jnp.int32, (tile_rows, columns), 0)
    first, last = row == 0, row == tile_rows - 1
    place = lax.broadcasted_iota(jnp.int32, (tile_rows, columns), 1).astype(jnp.float32)
    coriolis = coriolis_mid + coriolis_slope * (place / columns - 0.5)
    half = 0.5 * time_step

    def rows_inside(field):
        ahead = jnp.where(last, 0.0, pltpu.roll(field, tile_rows - 1, axis=0))
        behind = jnp.where(first, 0.0, pltpu.roll(field, 1, axis=0))
        return ahead - behind

    def cols(field):
        return pltpu.roll(field, columns - 1, axis=1) - pltpu.roll(field, 1, axis=1)

    def mixed(fields, m):
        return sum(coupling[l][m] * fields[l] for l in range(3))

    goes_on = jnp.where(lax.axis_index("tm") == lax.axis_size("tm") - 1, 0, 1)

    def started(number):
        return jnp.where(goes_on > 0, adjoint_ref[number], 0.0)

    copies = [spill_copy, depth_copy]
    for turn in range(STEPS):
        step = STEPS - 1 - turn
        state = started if turn == 0 else out_ref.__getitem__
        height = [state(l) + forcing_ref[step * layers + l] for l in range(layers)]
        if turn > 0:
            for l in range(layers):
                number = step * layers + l
                height[l] += jnp.where(first, spill_in[number : number + 1, :], 0.0)
        east = [state(layers + l) for l in range(layers)]
        north = [state(2 * layers + l) for l in range(layers)]
        east_mix = [mixed(east, m) for m in range(layers)]
        for l in range(layers):
            thick = depth_ref[l] * height[l]
            edge_out[turn, 0, l : l + 1, :] = thick[0:1, :]
            edge_out[turn, 1, l : l + 1, :] = thick[tile_rows - 1 :, :]
            edge_out[turn, 0, layers + l : layers + l + 1, :] = east_mix[l][0:1, :]
            edge_out[turn, 1, layers + l : layers + l + 1, :] = east_mix[l][tile_rows - 1 :, :]
        to_before = copy(edge_out.at[turn, 0], edge_in.at[turn, 0], 2 * turn, before)
        to_after = copy(edge_out.at[turn, 1], edge_in.at[turn, 1], 2 * turn + 1, after)
        to_before.start()
        to_after.start()
        copies += [to_before, to_after]
        if turn == 0:
            spill_copy.wait_recv()
            for l in range(layers):
                number = step * layers + l
                height[l] += jnp.where(first, spill_in[number : number + 1, :], 0.0)
        for l in range(layers):
            thick = depth_ref[l] * height[l]
            north_mix = mixed(north, l)
            out_ref[l] = height[l] + half * (rows_inside(east_mix[l]) + cols(north_mix))
            out_ref[layers + l] = (
                east[l]
                + half * rows_inside(thick)
                - time_step * (coriolis * north[l] + friction * east[l])
            )
            out_ref[2 * layers + l] = (
                north[l]
                + half * cols(thick)
                + time_step * (coriolis * east[l] - friction * north[l])
            )
        to_before.wait_recv()
        to_after.wait_recv()
        if turn == 0:
            depth_copy.wait_recv()
        for l in range(layers):
            below = edge_in[turn, 0, l : l + 1, :]
            if turn == 0:
                number = step * layers + l
                below += depth_in[l : l + 1, :] * spill_ref[number : number + 1, :]
            above = edge_in[turn, 1, l : l + 1, :]
            below_mix = edge_in[turn, 0, layers + l : layers + l + 1, :]
            above_mix = edge_in[turn, 1, layers + l : layers + l + 1, :]
            out_ref[l, 0:1, :] += -half * above_mix
            out_ref[l, tile_rows - 1 :, :] += half * below_mix
            out_ref[layers + l, 0:1, :] += -half * above
            out_ref[layers + l, tile_rows - 1 :, :] += half * below
    for one in copies:
        one.wait_send()


def stencil(adjoint, depth, forcing, spill):
    layers, tile_rows, columns = depth.shape
    planes = forcing.shape[0]
    vmem = pl.BlockSpec(memory_space=pltpu.VMEM)
    return pl.pallas_call(
        stencil_kernel,
        out_shape=jax.ShapeDtypeStruct((3 * layers, tile_rows, columns), jnp.float32),
        in_specs=[vmem] * 4,
        out_specs=vmem,
        scratch_shapes=[
            pltpu.VMEM((STEPS, 2, 2 * layers, columns), jnp.float32),
            pltpu.VMEM((STEPS, 2, 2 * layers, columns), jnp.float32),
            pltpu.VMEM((layers, columns), jnp.float32),
            pltpu.VMEM((layers, columns), jnp.float32),
            pltpu.VMEM((planes, columns), jnp.float32),
            pltpu.SemaphoreType.DMA((2 * STEPS + 2,)),
            pltpu.SemaphoreType.DMA((2 * STEPS + 2,)),
        ],
        compiler_params=pltpu.CompilerParams(
            collective_id=0, has_side_effects=True, vmem_limit_bytes=32 * 1024 * 1024
        ),
        name="stencil",
    )(adjoint, depth, forcing, spill)


def body(
    adjoint_in, layer_depth, obs_cell, obs_plane, obs_owner, innovation, obs_weight, obs_count
):
    tiles = lax.axis_size("space")
    layer_count = layer_depth.shape[0]
    tile_rows = layer_depth.shape[1]
    columns = layer_depth.shape[2]
    obs_rows = obs_cell.shape[1]
    capacity = 5 * obs_rows // (4 * tiles)
    planes = STEPS * layer_count
    lines = obs_rows // LANES
    adjoint = adjoint_in[0].reshape(3 * layer_count, tile_rows, columns)
    arrived, following = route(
        obs_cell.reshape(lines, LANES),
        obs_plane.reshape(lines, LANES),
        obs_owner.reshape(lines, LANES),
        innovation.reshape(lines, LANES),
        obs_weight.reshape(4, lines, LANES),
        obs_count,
        adjoint,
        tiles,
        capacity,
        columns,
        tile_rows,
    )
    forcing, spill = force(arrived, planes, tile_rows, columns)
    current = stencil(following, layer_depth, forcing, spill)
    result = adjoint_in[0] - current.reshape(3, layer_count, tile_rows, columns)
    return result[None]


def solution(mesh):
    in_specs = (
        P(("ens", "tm"), None, None, "space", None),
        P(None, "space", None),
        P(("ens", "tm"), "space"),
        P(("ens", "tm"), "space"),
        P(("ens", "tm"), "space", None),
        P(("ens", "tm"), "space"),
        P(None, ("ens", "tm"), "space"),
        P(("ens", "tm"), "space"),
    )
    out_specs = P(("ens", "tm"), None, None, "space", None)
    return jax.shard_map(body, mesh=mesh, in_specs=in_specs, out_specs=out_specs, check_vma=False)
```

```python
import functools

import jax
import jax.numpy as jnp
from jax import lax
from jax.experimental import pallas as pl
from jax.experimental.pallas import tpu as pltpu
from jax.sharding import PartitionSpec as P

STEPS = 4
LANES = 128
WINDOW = 256
FIELDS = 6
GROUP = 8

time_step = 0.4
friction = 0.05
coriolis_mid = 0.3
coriolis_slope = 0.2
coupling = ((1.0, 0.5, 0.25), (0.5, 1.0, 0.5), (0.25, 0.5, 1.0))

NT = (((1,), (1,)), ((), ()))


def spread(row, rows):
    part = jnp.broadcast_to(row, (16, row.shape[1])).astype(jnp.bfloat16)
    return jnp.concatenate([part] * (rows // 16), axis=0)


def one_hot(index_row, rows):
    places = lax.broadcasted_iota(jnp.int32, (rows, index_row.shape[1]), 0)
    return jnp.where(places == index_row, 1.0, 0.0)


def one_hot_16(index_row, rows):
    places = lax.broadcasted_iota(jnp.int32, (rows, index_row.shape[1]), 0)
    places = places.astype(jnp.float32).astype(jnp.bfloat16)
    same = places == spread(index_row.astype(jnp.float32), rows)
    return jnp.where(same, jnp.bfloat16(1), jnp.bfloat16(0))


def route_kernel(
    tiles,
    capacity,
    columns,
    tile_rows,
    width,
    count_ref,
    cell_hbm,
    plane_hbm,
    owner_hbm,
    innov_hbm,
    weight_hbm,
    adjoint_hbm,
    out_ref,
    following_hbm,
    cell_ref,
    plane_ref,
    owner_ref,
    innov_ref,
    weight_ref,
    key_ref,
    pos_ref,
    piece_ref,
    hit_ref,
    acc_ref,
    slab_ref,
    load_sem,
    send_sem,
    recv_sem,
):
    loads = [
        pltpu.make_async_copy(source, target, load_sem.at[number])
        for number, (source, target) in enumerate(
            [
                (cell_hbm, cell_ref),
                (owner_hbm, owner_ref),
                (plane_hbm, plane_ref),
                (innov_hbm, innov_ref),
                (weight_hbm, weight_ref),
            ]
        )
    ]
    for load in loads:
        load.start()
    me = lax.axis_index("space")
    window = lax.axis_index("tm")
    windows = lax.axis_size("tm")
    half = tiles // 2
    local = lax.rem(me, half)
    my_base = me - local
    other_base = half - my_base
    barrier = pltpu.get_barrier_semaphore()
    for distance in range(1, tiles):
        pl.semaphore_signal(
            barrier,
            inc=1,
            device_id={"space": lax.rem(me + distance, tiles)},
            device_id_type=pl.DeviceIdType.MESH,
        )
    earlier_window = lax.rem(window + windows - 1, windows)
    for distance in range(1, windows):
        pl.semaphore_signal(
            barrier,
            inc=1,
            device_id={"tm": lax.rem(window + distance, windows)},
            device_id_type=pl.DeviceIdType.MESH,
        )
    pl.semaphore_wait(barrier, tiles - 1 + windows - 1)
    follow = pltpu.make_async_remote_copy(
        src_ref=adjoint_hbm,
        dst_ref=following_hbm,
        send_sem=send_sem.at[tiles],
        recv_sem=recv_sem.at[tiles],
        device_id={"tm": earlier_window},
        device_id_type=pl.DeviceIdType.MESH,
    )
    follow.start()
    for load in loads:
        load.wait()
    lines = cell_ref.shape[0]
    buckets = columns // WINDOW
    keys = tiles * buckets
    slot_rows = tiles * capacity // width
    place = lax.broadcasted_iota(jnp.int32, (lines, LANES), 0) * LANES + lax.broadcasted_iota(
        jnp.int32, (lines, LANES), 1
    )
    live = place < count_ref[0, 0]
    cell = cell_ref[...]
    column = jnp.bitwise_and(cell, columns - 1)
    row = jnp.right_shift(cell, columns.bit_length() - 1)
    bucket = jnp.right_shift(column, WINDOW.bit_length() - 1)
    key_ref[...] = jnp.where(live, owner_ref[...] * buckets + bucket, keys)
    piece_ref[0] = (plane_ref[...] * tile_rows + row + 1).astype(jnp.float32)
    piece_ref[1] = (bucket * WINDOW).astype(jnp.float32)
    piece_ref[2] = jnp.bitwise_and(column, WINDOW - 1).astype(jnp.float32)
    innovation = innov_ref[...]
    for corner in range(4):
        value = weight_ref[corner] * innovation
        high = value.astype(jnp.bfloat16).astype(jnp.float32)
        piece_ref[3 + 2 * corner] = high
        piece_ref[4 + 2 * corner] = value - high

    def count_step(line, total):
        for extra in range(8):
            total += one_hot(key_ref[pl.ds(line * 8 + extra, 1), :], keys)
        return total

    total = lax.fori_loop(0, lines // 8, count_step, jnp.zeros((keys, LANES), jnp.float32))
    mine = lax.broadcasted_iota(jnp.int32, (keys, keys), 0)
    other = lax.broadcasted_iota(jnp.int32, (keys, keys), 1)
    shift = buckets.bit_length() - 1
    same_owner = jnp.right_shift(mine, shift) == jnp.right_shift(other, shift)
    before = jnp.where(same_owner & (other < mine), 1.0, 0.0).astype(jnp.bfloat16)
    ahead = jnp.dot(before, total.astype(jnp.bfloat16), preferred_element_type=jnp.float32)
    owner_of = jnp.right_shift(lax.broadcasted_iota(jnp.int32, (keys, 1), 0), shift)
    base = jnp.sum(ahead, axis=1, keepdims=True) + (owner_of * capacity).astype(jnp.float32)
    triangle = jnp.where(
        lax.broadcasted_iota(jnp.int32, (256, 256), 0)
        < lax.broadcasted_iota(jnp.int32, (256, 256), 1),
        1.0,
        0.0,
    ).astype(jnp.bfloat16)

    def rank_step(step, base):
        for extra in range(4):
            line = step * 8 + extra * 2
            key = jnp.concatenate(
                [key_ref[pl.ds(line, 1), :], key_ref[pl.ds(line + 1, 1), :]], axis=1
            )
            hits = one_hot(key, keys)
            earlier = jnp.dot(
                hits.astype(jnp.bfloat16), triangle, preferred_element_type=jnp.float32
            )
            position = jnp.sum(hits * (earlier + base), axis=0, keepdims=True).astype(jnp.int32)
            position = jnp.where(key < keys, position, -1)
            pos_ref[pl.ds(line, 1), :] = position[:, :LANES]
            pos_ref[pl.ds(line + 1, 1), :] = position[:, LANES:]
            base += jnp.sum(hits, axis=1, keepdims=True)
        return base

    lax.fori_loop(0, lines // 8, rank_step, base)
    log_width = width.bit_length() - 1
    half_rows = slot_rows // 2
    part_rows = (half_rows + 15) // 16 * 16
    per_owner = capacity // width
    per_half = tiles // 2
    span = range(8)

    def move_half(first_row, fresh):
        acc_ref[...] = jnp.zeros_like(acc_ref)

        def move_step(step, carry):
            parts, lefts = [], []
            for extra in span:
                position = pos_ref[pl.ds(step * 8 + extra, 1), :]
                slot = jnp.right_shift(position, log_width) - first_row
                slots = one_hot_16(slot, part_rows)
                pieces = [
                    slots * spread(piece_ref[piece, pl.ds(step * 8 + extra, 1), :], part_rows)
                    for piece in range(11)
                ]
                parts.append(jnp.concatenate(pieces, axis=0))
                if fresh:
                    lane = jnp.bitwise_and(position, width - 1)
                    lefts.append(one_hot_16(lane, width))
            if fresh:
                lane_hits = jnp.concatenate(lefts, axis=1)
                hit_ref[step] = lane_hits
            else:
                lane_hits = hit_ref[step]
            acc_ref[...] += lax.dot_general(
                jnp.concatenate(parts, axis=1), lane_hits, NT, preferred_element_type=jnp.float32
            )
            return carry

        lax.fori_loop(0, lines // 8, move_step, 0)
        for owner in range(per_half):
            for field in range(FIELDS):

                def piece_rows(piece):
                    first = piece * part_rows + owner * per_owner
                    return acc_ref[first : first + per_owner, :]

                value = piece_rows(0)
                if field > 0:
                    value = piece_rows(2 * field - 1) + piece_rows(2 * field)
                target = slice(field * per_owner, (field + 1) * per_owner)
                slab_ref[0 if fresh else 1, owner, target, :] = value

    def exchange(base, group, number):
        to_local = lax.rem(local + number, half)
        from_tile = base + lax.rem(local + half - number, half)

        def copy(slot):
            return pltpu.make_async_remote_copy(
                src_ref=slab_ref.at[group, to_local],
                dst_ref=out_ref.at[slot],
                send_sem=send_sem.at[group * half + number],
                recv_sem=recv_sem.at[group * half + number],
                device_id={"space": base + to_local},
                device_id_type=pl.DeviceIdType.MESH,
            )

        return copy(me), copy(from_tile)

    pairs = []
    move_half(other_base * per_owner, True)
    for number in range(half):
        pairs.append(exchange(other_base, 0, number))
        pairs[-1][0].start()
    move_half(my_base * per_owner, False)
    for number in range(1, half):
        pairs.append(exchange(my_base, 1, number))
        pairs[-1][0].start()
    out_ref[me] = slab_ref[1, local]
    for sent, got in pairs:
        got.wait_recv()
    follow.wait_recv()
    for sent, got in pairs:
        sent.wait_send()
    follow.wait_send()


def route(
    cell, plane, owner, innov, weights, count, adjoint, tiles, capacity, columns, tile_rows
):
    lines = cell.shape[0]
    width = 256 if capacity % 256 == 0 else LANES
    half_rows = tiles * capacity // width // 2
    part_rows = (half_rows + 15) // 16 * 16
    depth = FIELDS * (capacity // width)
    vmem = pl.BlockSpec(memory_space=pltpu.VMEM)
    anywhere = pl.BlockSpec(memory_space=pltpu.HBM)
    whole = pltpu.VMEM((lines, LANES), jnp.int32)
    return pl.pallas_call(
        functools.partial(route_kernel, tiles, capacity, columns, tile_rows, width),
        out_shape=(
            jax.ShapeDtypeStruct((tiles, depth, width), jnp.float32),
            jax.ShapeDtypeStruct(adjoint.shape, adjoint.dtype),
        ),
        in_specs=[pl.BlockSpec(memory_space=pltpu.SMEM)] + [anywhere] * 6,
        out_specs=(vmem, anywhere),
        scratch_shapes=[
            whole,
            whole,
            whole,
            pltpu.VMEM((lines, LANES), jnp.float32),
            pltpu.VMEM((4, lines, LANES), jnp.float32),
            whole,
            whole,
            pltpu.VMEM((11, lines, LANES), jnp.float32),
            pltpu.VMEM((lines // 8, width, 8 * LANES), jnp.bfloat16),
            pltpu.VMEM((11 * part_rows, width), jnp.float32),
            pltpu.VMEM((2, tiles // 2, depth, width), jnp.float32),
            pltpu.SemaphoreType.DMA((5,)),
            pltpu.SemaphoreType.DMA((tiles + 1,)),
            pltpu.SemaphoreType.DMA((tiles + 1,)),
        ],
        compiler_params=pltpu.CompilerParams(
            collective_id=1, has_side_effects=True, vmem_limit_bytes=62 * 1024 * 1024
        ),
        name="route",
    )(count, cell, plane, owner, innov, weights, adjoint)


def force_kernel(
    planes, tile_rows, columns, low_ref, high_ref, in_ref, out_ref, spill_ref, acc_ref, item_ref
):
    tiles, depth, width = in_ref.shape
    per_tile = depth // FIELDS
    cells = planes * tile_rows
    windows = columns // WINDOW
    acc_ref[...] = jnp.zeros_like(acc_ref)

    def list_source(source, count):
        def list_block(block, count):
            number = source * per_tile + block

            def list_window(window, count):
                item_ref[0, count] = source
                item_ref[1, count] = block
                item_ref[2, count] = window
                item_ref[3, count] = window
                return count + 1

            return lax.fori_loop(low_ref[number], high_ref[number] + 1, list_window, count)

        return lax.fori_loop(0, per_tile, list_block, count)

    count = lax.fori_loop(0, tiles, list_source, 0)
    for extra in range(GROUP):
        item_ref[0, count + extra] = 0
        item_ref[1, count + extra] = 0
        item_ref[2, count + extra] = windows
        item_ref[3, count + extra] = 0

    def product(item):
        source, block = item_ref[0, item], item_ref[1, item]

        def field(number):
            return in_ref[source, pl.ds(number * per_tile + block, 1), :]

        line = field(0).astype(jnp.int32) - 1
        column = field(1).astype(jnp.int32)
        line_hits = one_hot_16(line, cells)
        highs, lows = [], []
        for corner in range(4):
            value = field(2 + corner)
            high = value.astype(jnp.bfloat16).astype(jnp.float32)
            highs.append(line_hits * spread(high, cells))
            lows.append(line_hits * spread(value - high, cells))
        left = jnp.concatenate(
            [jnp.concatenate(highs, axis=0), jnp.concatenate(lows, axis=0)], axis=1
        )
        hits = one_hot_16(column - item_ref[2, item] * WINDOW, WINDOW)
        right = jnp.concatenate([hits, hits], axis=1)
        return lax.dot_general(left, right, NT, preferred_element_type=jnp.float32)

    def group_step(group, carry):
        found = [product(group * GROUP + extra) for extra in range(GROUP)]
        for extra in range(GROUP):
            acc_ref[item_ref[3, group * GROUP + extra]] += found[extra]
        return carry

    lax.fori_loop(0, (count + GROUP - 1) // GROUP, group_step, 0)
    row = lax.broadcasted_iota(jnp.int32, (tile_rows, columns), 0)
    for plane in range(planes):

        def gathered(corner):
            first = corner * cells + plane * tile_rows
            return jnp.concatenate(
                [acc_ref[w, first : first + tile_rows, :] for w in range(columns // WINDOW)],
                axis=1,
            )

        here = gathered(0) + pltpu.roll(gathered(1), 1, axis=1)
        below = gathered(2) + pltpu.roll(gathered(3), 1, axis=1)
        below = pltpu.roll(below, 1, axis=0)
        out_ref[plane] = here + jnp.where(row > 0, below, 0.0)
        spill_ref[plane : plane + 1, :] = below[0:1, :]


def force(arrived, planes, tile_rows, columns):
    tiles, depth, width = arrived.shape
    per_tile = depth // FIELDS
    line = arrived[:, :per_tile]
    column = arrived[:, per_tile : 2 * per_tile]
    low = jnp.min(jnp.where(line > 0, column, float(columns)), axis=2).reshape(tiles * per_tile)
    high = jnp.max(jnp.where(line > 0, column, -1.0), axis=2).reshape(tiles * per_tile)
    low = jnp.floor(low / WINDOW).astype(jnp.int32)
    high = jnp.floor(high / WINDOW).astype(jnp.int32)
    vmem = pl.BlockSpec(memory_space=pltpu.VMEM)
    smem = pl.BlockSpec(memory_space=pltpu.SMEM)
    shape = jax.ShapeDtypeStruct((planes, tile_rows, columns), jnp.float32)
    return pl.pallas_call(
        functools.partial(force_kernel, planes, tile_rows, columns),
        out_shape=(shape, jax.ShapeDtypeStruct((planes, columns), jnp.float32)),
        in_specs=[smem, smem, vmem],
        out_specs=(vmem, vmem),
        scratch_shapes=[
            pltpu.VMEM((columns // WINDOW, 4 * planes * tile_rows, WINDOW), jnp.float32),
            pltpu.SMEM((4, tiles * (per_tile * 2 + 2 * columns // WINDOW) + GROUP), jnp.int32),
        ],
        compiler_params=pltpu.CompilerParams(vmem_limit_bytes=48 * 1024 * 1024),
        name="force",
    )(low, high, arrived)


def stencil_kernel(
    adjoint_ref,
    depth_ref,
    forcing_ref,
    spill_ref,
    out_ref,
    edge_out,
    edge_in,
    depth_out,
    depth_in,
    spill_in,
    send_sem,
    recv_sem,
):
    layers, tile_rows, columns = depth_ref.shape
    tiles = lax.axis_size("space")
    me = lax.axis_index("space")
    after = lax.rem(me + 1, tiles)
    before = lax.rem(me + tiles - 1, tiles)
    barrier = pltpu.get_barrier_semaphore()
    for neighbour in (before, after):
        pl.semaphore_signal(
            barrier,
            inc=1,
            device_id={"space": neighbour},
            device_id_type=pl.DeviceIdType.MESH,
        )
    pl.semaphore_wait(barrier, 2)

    def copy(source, target, number, neighbour):
        return pltpu.make_async_remote_copy(
            src_ref=source,
            dst_ref=target,
            send_sem=send_sem.at[number],
            recv_sem=recv_sem.at[number],
            device_id={"space": neighbour},
            device_id_type=pl.DeviceIdType.MESH,
        )

    spill_copy = copy(spill_ref, spill_in, 2 * STEPS, after)
    depth_copy = copy(depth_out, depth_in, 2 * STEPS + 1, before)
    spill_copy.start()
    for layer in range(layers):
        depth_out[layer : layer + 1, :] = depth_ref[layer, 0:1, :]
    depth_copy.start()

    row = lax.broadcasted_iota(jnp.int32, (tile_rows, columns), 0)
    first, last = row == 0, row == tile_rows - 1
    place = lax.broadcasted_iota(jnp.int32, (tile_rows, columns), 1).astype(jnp.float32)
    coriolis = coriolis_mid + coriolis_slope * (place / columns - 0.5)
    half = 0.5 * time_step

    def rows_inside(field):
        ahead = jnp.where(last, 0.0, pltpu.roll(field, tile_rows - 1, axis=0))
        behind = jnp.where(first, 0.0, pltpu.roll(field, 1, axis=0))
        return ahead - behind

    def cols(field):
        return pltpu.roll(field, columns - 1, axis=1) - pltpu.roll(field, 1, axis=1)

    def mixed(fields, m):
        return sum(coupling[l][m] * fields[l] for l in range(3))

    goes_on = jnp.where(lax.axis_index("tm") == lax.axis_size("tm") - 1, 0, 1)

    def started(number):
        return jnp.where(goes_on > 0, adjoint_ref[number], 0.0)

    copies = [spill_copy, depth_copy]
    for turn in range(STEPS):
        step = STEPS - 1 - turn
        state = started if turn == 0 else out_ref.__getitem__
        height = [state(l) + forcing_ref[step * layers + l] for l in range(layers)]
        if turn > 0:
            for l in range(layers):
                number = step * layers + l
                height[l] += jnp.where(first, spill_in[number : number + 1, :], 0.0)
        east = [state(layers + l) for l in range(layers)]
        north = [state(2 * layers + l) for l in range(layers)]
        east_mix = [mixed(east, m) for m in range(layers)]
        for l in range(layers):
            thick = depth_ref[l] * height[l]
            edge_out[turn, 0, l : l + 1, :] = thick[0:1, :]
            edge_out[turn, 1, l : l + 1, :] = thick[tile_rows - 1 :, :]
            edge_out[turn, 0, layers + l : layers + l + 1, :] = east_mix[l][0:1, :]
            edge_out[turn, 1, layers + l : layers + l + 1, :] = east_mix[l][tile_rows - 1 :, :]
        to_before = copy(edge_out.at[turn, 0], edge_in.at[turn, 0], 2 * turn, before)
        to_after = copy(edge_out.at[turn, 1], edge_in.at[turn, 1], 2 * turn + 1, after)
        to_before.start()
        to_after.start()
        copies += [to_before, to_after]
        if turn == 0:
            spill_copy.wait_recv()
            for l in range(layers):
                number = step * layers + l
                height[l] += jnp.where(first, spill_in[number : number + 1, :], 0.0)
        for l in range(layers):
            thick = depth_ref[l] * height[l]
            north_mix = mixed(north, l)
            out_ref[l] = height[l] + half * (rows_inside(east_mix[l]) + cols(north_mix))
            out_ref[layers + l] = (
                east[l]
                + half * rows_inside(thick)
                - time_step * (coriolis * north[l] + friction * east[l])
            )
            out_ref[2 * layers + l] = (
                north[l]
                + half * cols(thick)
                + time_step * (coriolis * east[l] - friction * north[l])
            )
        to_before.wait_recv()
        to_after.wait_recv()
        if turn == 0:
            depth_copy.wait_recv()
        for l in range(layers):
            below = edge_in[turn, 0, l : l + 1, :]
            if turn == 0:
                number = step * layers + l
                below += depth_in[l : l + 1, :] * spill_ref[number : number + 1, :]
            above = edge_in[turn, 1, l : l + 1, :]
            below_mix = edge_in[turn, 0, layers + l : layers + l + 1, :]
            above_mix = edge_in[turn, 1, layers + l : layers + l + 1, :]
            out_ref[l, 0:1, :] += -half * above_mix
            out_ref[l, tile_rows - 1 :, :] += half * below_mix
            out_ref[layers + l, 0:1, :] += -half * above
            out_ref[layers + l, tile_rows - 1 :, :] += half * below
    for one in copies:
        one.wait_send()


def stencil(adjoint, depth, forcing, spill):
    layers, tile_rows, columns = depth.shape
    planes = forcing.shape[0]
    vmem = pl.BlockSpec(memory_space=pltpu.VMEM)
    return pl.pallas_call(
        stencil_kernel,
        out_shape=jax.ShapeDtypeStruct((3 * layers, tile_rows, columns), jnp.float32),
        in_specs=[vmem] * 4,
        out_specs=vmem,
        scratch_shapes=[
            pltpu.VMEM((STEPS, 2, 2 * layers, columns), jnp.float32),
            pltpu.VMEM((STEPS, 2, 2 * layers, columns), jnp.float32),
            pltpu.VMEM((layers, columns), jnp.float32),
            pltpu.VMEM((layers, columns), jnp.float32),
            pltpu.VMEM((planes, columns), jnp.float32),
            pltpu.SemaphoreType.DMA((2 * STEPS + 2,)),
            pltpu.SemaphoreType.DMA((2 * STEPS + 2,)),
        ],
        compiler_params=pltpu.CompilerParams(
            collective_id=0, has_side_effects=True, vmem_limit_bytes=32 * 1024 * 1024
        ),
        name="stencil",
    )(adjoint, depth, forcing, spill)


def body(
    adjoint_in, layer_depth, obs_cell, obs_plane, obs_owner, innovation, obs_weight, obs_count
):
    tiles = lax.axis_size("space")
    layer_count = layer_depth.shape[0]
    tile_rows = layer_depth.shape[1]
    columns = layer_depth.shape[2]
    obs_rows = obs_cell.shape[1]
    capacity = 5 * obs_rows // (4 * tiles)
    planes = STEPS * layer_count
    lines = obs_rows // LANES
    adjoint = adjoint_in[0].reshape(3 * layer_count, tile_rows, columns)
    arrived, following = route(
        obs_cell.reshape(lines, LANES),
        obs_plane.reshape(lines, LANES),
        obs_owner.reshape(lines, LANES),
        innovation.reshape(lines, LANES),
        obs_weight.reshape(4, lines, LANES),
        obs_count,
        adjoint,
        tiles,
        capacity,
        columns,
        tile_rows,
    )
    forcing, spill = force(arrived, planes, tile_rows, columns)
    current = stencil(following, layer_depth, forcing, spill)
    result = adjoint_in[0] - current.reshape(3, layer_count, tile_rows, columns)
    return result[None]


def solution(mesh):
    in_specs = (
        P(("ens", "tm"), None, None, "space", None),
        P(None, "space", None),
        P(("ens", "tm"), "space"),
        P(("ens", "tm"), "space"),
        P(("ens", "tm"), "space", None),
        P(("ens", "tm"), "space"),
        P(None, ("ens", "tm"), "space"),
        P(("ens", "tm"), "space"),
    )
    out_specs = P(("ens", "tm"), None, None, "space", None)
    return jax.shard_map(body, mesh=mesh, in_specs=in_specs, out_specs=out_specs, check_vma=False)
```
